256 devices in a mesh: dp: 64 (over x, z, y_hi), seq: 4 (over y_lo, core).
Axes of the slice: x: 4, y: 4 (y_hi: 2, y_lo: 2; y = y_hi * 2 + y_lo), z: 8, core: 2. Of those that a mesh axis runs over, the one named last changes fastest.
Arguments:
- layer_input: bfloat16 [64, 512, 5120], P('dp', 'seq'), may hold values from -16 to 16
- query_states: bfloat16 [64, 512, 2560], P('dp', 'seq'), may hold values from -7 to 7
- key_states: bfloat16 [64, 512, 512], P('dp', 'seq'), may hold values from -7 to 7
- value_states: bfloat16 [64, 512, 512], P('dp', 'seq'), may hold values from -6 to 6
- output_grads: bfloat16 [64, 512, 2560], P('dp', 'seq'), may hold values from -24 to 24
- doc_lengths: int32 [64, 6], P('dp'), may hold values from 1 to 256, 512 in all within a row
Outputs:
- query_grads: bfloat16 [64, 512, 2560], P('dp', 'seq')
- key_weight_grads: float32 [5120, 512], P('dp', 'seq')
- value_weight_grads: float32 [5120, 512], P('dp', 'seq')
The draws below stay inside these ranges and needn't reach their ends.
Inputs may be any that keep to these rules, and one draw needn't show every extreme that they name: `doc_lengths`: each row holds the lengths of the 6 documents of one sequence in order; they sum to 512 and the longest has exactly 256 tokens.
All inputs are finite; a program needn't handle non-finite values.
Results may differ from the reference program's by a relative error of at most 0.018.
Values may be sent and summed in bfloat16 or wider, within the bound.
A program may use at most 128 MiB of HBM per device.

```python
import math
from functools import partial
import jax
import jax.numpy as jnp
import numpy as np
from jax import lax

D = 5120
HD = 128
KVH = 4
GROUP = 5
HQ = 20
SEQ_LEN = 512
SEQS = 64
NDOCS = 6
MOST_DOC = 256


def draw_query_states(key, part):
    key = jax.random.fold_in(key, 11)
    drawn = jnp.clip(jax.random.normal(key, (SEQS, SEQ_LEN, KVH, GROUP, HD), jnp.float32), -6.0, 6.0)
    return drawn.reshape(SEQS, SEQ_LEN, KVH * GROUP * HD).astype(jnp.bfloat16)


def draw_key_states(key, part):
    key = jax.random.fold_in(key, 12)
    drawn = jnp.clip(jax.random.normal(key, (SEQS, SEQ_LEN, KVH, HD), jnp.float32), -6.0, 6.0)
    return drawn.reshape(SEQS, SEQ_LEN, KVH * HD).astype(jnp.bfloat16)


def raised(values, rng, source, target, parts, factor):
    owner, partner = [(jnp.arange(values.shape[position]) // (values.shape[position] // parts)).reshape([-1 if axis == position else 1 for axis in range(values.ndim)]) for position in (source, target)]
    chosen = jax.random.permutation(rng, parts)[partner]
    strong = (owner == chosen) | (owner == (partner + parts // 2) % parts)
    return jnp.where(strong, factor * values, values)


def level_of(own_key, dims, cuts, smallest, top_value):
    def one(axis_at, blocks):
        steps = jax.random.uniform(jax.random.fold_in(jax.random.fold_in(own_key, 6), axis_at), (blocks,), jnp.float32, smallest / len(cuts), top_value / len(cuts))
        return jnp.repeat(jnp.exp(steps), dims[axis_at] // blocks).reshape((-1,) + (1,) * (len(dims) - axis_at - 1))

    level = one(*cuts[0])
    for cut in cuts[1:]:
        level = level * one(*cut)
    return level


def split_up(number_of, total, limit, skew):
    loads = [(1 << 20) // math.isqrt(grade ** skew) + 1 for grade in range(2, number_of + 1)]
    rest, holding = total - limit - (number_of - 1), [1] * (number_of - 1)
    while rest > 0:
        free = [i for i in range(number_of - 1) if holding[i] < limit]
        pool, left = sum([loads[i] for i in free]), rest
        for i in free:
            extra = min(limit - holding[i], max(1, left * loads[i] // pool), rest)
            holding[i] = holding[i] + extra
            rest = rest - extra
    return np.array([limit] + holding)


def uneven(rng, amount, total, bound, lean):
    if amount == 2:
        one = jax.random.randint(rng, (), max(1, total - bound), min(bound, total - 1) + 1)
        return jnp.stack([one, total - one])
    lengths = jnp.asarray(split_up(amount, total, bound, lean), jnp.int32)
    pairs = (amount - 1) // 2
    donor, sink = lengths[1:1 + 2 * pairs:2], lengths[2:2 + 2 * pairs:2]
    margin = jnp.minimum(donor - 1, bound - sink)
    passed = jax.random.randint(jax.random.fold_in(rng, 1), (pairs,), 0, 1 << 20) % (margin + 1)
    lengths = lengths.at[1:1 + 2 * pairs:2].set(donor - passed).at[2:2 + 2 * pairs:2].set(sink + passed)
    return lengths[jax.random.permutation(jax.random.fold_in(rng, 2), amount)]


def scatter_about(key, extent, deviation, bound, split=(), kind=jnp.bfloat16):
    values = jax.random.normal(key, extent, jnp.float32) * deviation
    if len(split) > 0:
        values = level_of(key, extent, split, -0.22, 0.18) * values
    return jnp.clip(values, min=-bound, max=bound).astype(kind)


def noise_with(key, dims, width, limit, pieces, heavy, kind=jnp.bfloat16):
    result = width * jax.random.normal(key, dims, jnp.float32)
    if pieces:
        result = result * level_of(key, dims, pieces, -0.22, 0.18)
    return jnp.clip(raised(result, jax.random.fold_in(key, 3), *heavy), -limit, limit).astype(kind)


def setup_inputs(seed: int = 0) -> dict:
    key_of = jax.random.split(jax.random.key(seed), 7)
    return {
        "layer_input": noise_with(key_of[0], (SEQS, SEQ_LEN, D), 1.0, 16.0, ((0, 64), (1, 4)), (0, 2, 64, 4.0)),
        "query_states": draw_query_states(jax.random.fold_in(key_of[6], 71), 0),
        "key_states": draw_key_states(jax.random.fold_in(key_of[6], 71), 0),
        "value_states": scatter_about(key_of[3], (SEQS, SEQ_LEN, KVH * HD), 1.0, 6.0, ((0, 64), (1, 4))),
        "output_grads": scatter_about(key_of[4], (SEQS, SEQ_LEN, HQ * HD), 4.0, 24.0, ((0, 64), (1, 4))),
        "doc_lengths": jax.vmap(lambda own: uneven(own, NDOCS, SEQ_LEN, MOST_DOC, 2))(jax.random.split(key_of[5], SEQS)).reshape((SEQS, NDOCS)).astype(jnp.int32),
    }


NEG_FILL = -1.0e30


def document_ids(length_row, count):
    doc_ends = jnp.cumsum(length_row.astype(jnp.int32)).astype(jnp.int32)
    positions = jnp.arange(count, dtype=jnp.int32)
    return jnp.sum((positions[:, None] >= doc_ends[None, :]).astype(jnp.int32), axis=1)


def group_backward(operands, allowed):
    query_group, key_group, value_group, grad_group = operands
    score_scale = HD ** -0.5
    scores = jnp.einsum("qhd,kd->hqk", query_group.astype(jnp.float32), key_group.astype(jnp.float32)) * score_scale
    scores = jnp.where(allowed[None], scores, NEG_FILL)
    row_max = jnp.max(scores, axis=-1, keepdims=True)
    shifted = jnp.exp(scores - row_max)
    probabilities = shifted / jnp.sum(shifted, axis=-1, keepdims=True)
    prob_bf = probabilities.astype(jnp.bfloat16)
    dprobs = jnp.einsum("qhd,kd->hqk", grad_group.astype(jnp.float32), value_group.astype(jnp.float32))
    row_delta = jnp.sum(probabilities * dprobs, axis=-1, keepdims=True)
    dscores = (probabilities * (dprobs - row_delta) * score_scale).astype(jnp.bfloat16)
    query_grad = jnp.einsum("hqk,kd->qhd", dscores.astype(jnp.float32), key_group.astype(jnp.float32)).astype(jnp.bfloat16)
    key_grad = jnp.einsum("hqk,qhd->kd", dscores.astype(jnp.float32), query_group.astype(jnp.float32)).astype(jnp.bfloat16)
    value_grad = jnp.einsum("hqk,qhd->kd", prob_bf.astype(jnp.float32), grad_group.astype(jnp.float32)).astype(jnp.bfloat16)
    return query_grad, key_grad, value_grad


def reference(layer_input, query_states, key_states, value_states, output_grads, doc_lengths):
    positions = jnp.arange(SEQ_LEN, dtype=jnp.int32)
    causal = positions[None, :] <= positions[:, None]

    def one_sequence(running, sequence):
        inputs_row, query_row, key_row, value_row, grad_row, length_row = sequence
        documents = document_ids(length_row, SEQ_LEN)
        allowed = (documents[:, None] == documents[None, :]) & causal
        grouped = (jnp.moveaxis(query_row.reshape(SEQ_LEN, KVH, GROUP, HD), 1, 0),
                   jnp.moveaxis(key_row.reshape(SEQ_LEN, KVH, HD), 1, 0),
                   jnp.moveaxis(value_row.reshape(SEQ_LEN, KVH, HD), 1, 0),
                   jnp.moveaxis(grad_row.reshape(SEQ_LEN, KVH, GROUP, HD), 1, 0))
        query_grad, key_grad, value_grad = lax.map(partial(group_backward, allowed=allowed), grouped)
        query_grad = jnp.moveaxis(query_grad, 0, 1).reshape(SEQ_LEN, KVH * GROUP * HD)
        key_grad = jnp.moveaxis(key_grad, 0, 1).reshape(SEQ_LEN, KVH * HD)
        value_grad = jnp.moveaxis(value_grad, 0, 1).reshape(SEQ_LEN, KVH * HD)
        key_total = running[0] + jnp.dot(inputs_row.T, key_grad, preferred_element_type=jnp.float32)
        value_total = running[1] + jnp.dot(inputs_row.T, value_grad, preferred_element_type=jnp.float32)
        return (key_total, value_total), query_grad

    zeros_init = jnp.zeros((D, KVH * HD), jnp.float32)
    totals, query_grads = lax.scan(one_sequence, (zeros_init, zeros_init),
                                   (layer_input, query_states, key_states, value_states, output_grads, doc_lengths))
    return query_grads, totals[0] / SEQS, totals[1] / SEQS
```

```python
import jax
import jax.numpy as jnp
from jax import lax
from jax.experimental import pallas as pl
from jax.experimental.pallas import tpu as pltpu
from jax.sharding import PartitionSpec as P

HD = 128
KVH = 4
GROUP = 5
TOK = 128
D = 5120
XW = D // 4
NX, NY, NZ = 4, 4, 8
ROWS = 80
LOG2E = 1.4426950408889634
SCALE = HD ** (-0.5)
MESH = pl.DeviceIdType.MESH
F32 = jnp.float32
BF16 = jnp.bfloat16


def kernel(
    doc_ref, x_hbm, q_hbm, k_hbm, v_hbm, do_hbm,
    dq_hbm, wk_ref, wv_ref,
    xin, qin, doin, kv, bias, ds_s, pb_s, dq_s, xt_send, xt_all,
    part_own, part_send, part_recv, kvout, kv_all, dw, zsend, zrecv, ysend, yrecv,
    ld_sem, kv_ss, kv_rs, x_ss, x_rs, xf_ss, xf_rs, p_ss, p_rs,
    ag_ss, ag_rs, rl_ss, rl_rs, z_ss, z_rs, y_ss, y_rs, out_sem,
):
    dp = lax.axis_index("dp")
    sq = lax.axis_index("seq")
    x = dp // 16
    z = (dp // 2) % 8
    yh = dp % 2
    yl = sq // 2
    c = sq % 2
    y = yh * 2 + yl

    def dev(xx, yy, zz, cc):
        return ((xx * 8 + zz) * 2 + yy // 2, (yy % 2) * 2 + cc)

    def seq_dev(delta):
        return (dp, (sq + delta) % 4)

    def rcopy(src, dst, ss, rs, device):
        return pltpu.make_async_remote_copy(
            src_ref=src, dst_ref=dst, send_sem=ss, recv_sem=rs,
            device_id=device, device_id_type=MESH,
        )

    loads = []
    for h in range(KVH):
        for i, ref in enumerate((k_hbm, v_hbm)):
            loads.append(pltpu.make_async_copy(
                ref.at[:, h * HD:(h + 1) * HD], kv.at[h, i, 256:384], ld_sem.at[h * 2 + i]))
    load_x = pltpu.make_async_copy(x_hbm, xin, ld_sem.at[8])
    load_q = pltpu.make_async_copy(q_hbm, qin, ld_sem.at[9])
    load_do = pltpu.make_async_copy(do_hbm, doin, ld_sem.at[10])
    for cp in loads:
        cp.start()
    load_x.start()
    load_q.start()
    load_do.start()

    barrier = pltpu.get_barrier_semaphore()
    xp, xm = (x + 1) % NX, (x + 3) % NX
    zp, zm = (z + 1) % NZ, (z + 7) % NZ
    out_y = (y + 3 + 2 * yl) % NY
    peers = [
        seq_dev(1), seq_dev(2), seq_dev(3),
        dev(xp, y, z, c), dev(xp, y, z, 1 - c), dev(xm, y, z, c), dev(xm, y, z, 1 - c),
        dev((x + 2) % NX, y, z, c),
        dev(x, y, zp, c), dev(x, y, zm, c),
        dev(x, out_y, z, c), dev(x, (y + 2) % NY, z, c),
    ]
    for peer in peers:
        pl.semaphore_signal(barrier, inc=1, device_id=peer, device_id_type=MESH)

    rows = lax.broadcasted_iota(jnp.int32, (TOK, 1), 0) + sq * TOK
    start = jnp.zeros((TOK, 1), jnp.int32)
    end = jnp.int32(0)
    for n in range(6):
        end = end + doc_ref[0, n]
        start = jnp.where(rows >= end, end, start)
    cols = lax.broadcasted_iota(jnp.int32, (TOK, 384), 1) + (sq - 2) * TOK
    bias[...] = jnp.where((cols >= start) & (cols <= rows), 0.0, -1e30).astype(F32)

    for cp in loads:
        cp.wait()
    pl.semaphore_wait(barrier, len(peers))

    sends = []
    for h in range(KVH):
        for delta in (1, 2):
            cp = rcopy(kv.at[h, :, 256:384], kv.at[h, :, (2 - delta) * TOK:(3 - delta) * TOK],
                       kv_ss.at[h, delta - 1], kv_rs.at[h, delta - 1], seq_dev(delta))
            cp.start()
            sends.append(cp)

    load_x.wait()

    def xt_slot(ref, d, rel):
        return ref.at[:, (d * 2 + rel) * TOK:(d * 2 + rel + 1) * TOK]

    for d in (1, 3, 2, 0):
        target = (x + d) % NX

        def turn(i, _, d=d, target=target):
            col = pl.multiple_of(target * XW + i * 128, 128)
            row = pl.multiple_of(i * 128, 128)
            tile = xin[:, pl.ds(col, 128)].T
            if d == 0:
                xt_all[pl.ds(row, 128), 0:128] = tile
            else:
                xt_send[d - 1, pl.ds(row, 128), :] = tile
            return 0

        lax.fori_loop(0, XW // 128, turn, 0)
        if d > 0:
            cp = rcopy(xt_send.at[d - 1], xt_slot(xt_all, d, 0), x_ss.at[d - 1], x_rs.at[d - 1],
                       dev(target, y, z, c))
            cp.start()
            sends.append(cp)

    def x_forward(d):
        cp = rcopy(xt_slot(xt_all, d, 0), xt_slot(xt_all, d, 1), xf_ss.at[d], xf_rs.at[d],
                   dev(x, y, z, 1 - c))
        cp.start()
        sends.append(cp)

    x_forward(0)
    load_q.wait()
    load_do.wait()

    out_copies = []

    def attention(h):
        for delta in (1, 2):
            rcopy(kv.at[h, :, 256:384], kv.at[h, :, (2 - delta) * TOK:(3 - delta) * TOK],
                  kv_ss.at[h, delta - 1], kv_rs.at[h, delta - 1], seq_dev(delta)).wait_recv()

        def head(g, _):
            col = pl.multiple_of((h * GROUP + g) * HD, HD)
            row = pl.multiple_of(g * TOK, TOK)
            kk = kv[h, 0]
            vv = kv[h, 1]
            s = lax.dot_general(qin[:, pl.ds(col, HD)], kk, (((1,), (1,)), ((), ())),
                                preferred_element_type=F32)
            s = s * (SCALE * LOG2E) + bias[...]
            m = jnp.max(s, axis=1, keepdims=True)
            e = jnp.exp2(s - m)
            p = e * (1.0 / jnp.sum(e, axis=1, keepdims=True))
            dpr = lax.dot_general(doin[:, pl.ds(col, HD)], vv, (((1,), (1,)), ((), ())),
                                  preferred_element_type=F32)
            delta_r = jnp.sum(p * dpr, axis=1, keepdims=True)
            ds = (p * (dpr - delta_r) * SCALE).astype(BF16)
            ds_s[pl.ds(row, TOK), :] = ds
            pb_s[pl.ds(row, TOK), :] = p.astype(BF16)
            dq = jnp.dot(ds, kk, preferred_element_type=F32)
            dq_s[:, pl.ds(col, HD)] = dq.astype(BF16)
            return 0

        lax.fori_loop(0, GROUP, head, 0)
        width = GROUP * HD
        cp = pltpu.make_async_copy(dq_s.at[:, h * width:(h + 1) * width],
                                   dq_hbm.at[:, h * width:(h + 1) * width], out_sem.at[h])
        cp.start()
        out_copies.append(cp)
        for i, (src, grads) in enumerate(((qin, ds_s), (doin, pb_s))):
            stacked = jnp.concatenate(
                [src[:, (h * GROUP + g) * HD:(h * GROUP + g + 1) * HD] for g in range(GROUP)],
                axis=0)
            t = lax.dot_general(stacked, grads[...], (((0,), (0,)), ((), ())),
                                preferred_element_type=F32)
            part_own[h, i] = t[:, 256:384]
            part_send[h, 0, i] = t[:, 128:256].astype(BF16)
            part_send[h, 1, i] = t[:, 0:128].astype(BF16)
        for delta in (1, 2):
            cp = part_copy(h, delta)
            cp.start()
            sends.append(cp)

    def part_copy(h, delta):
        return rcopy(part_send.at[h, delta - 1], part_recv.at[h, delta - 1],
                     p_ss.at[h, delta - 1], p_rs.at[h, delta - 1], seq_dev(4 - delta))

    def ag_rows(slot):
        return pl.ds(pl.multiple_of(slot * TOK, TOK), TOK)

    def finalize(h):
        j, core = h // 2, h % 2
        rel = (c + h) % 2
        for delta in (1, 2):
            part_copy(h, delta).wait_recv()
        for i in range(2):
            total = (part_own[h, i] + part_recv[h, 0, i].astype(F32)
                     + part_recv[h, 1, i].astype(F32))
            kvout[h, :, i * HD:(i + 1) * HD] = total.T.astype(BF16)

        for n, (d, xx) in enumerate(((1, xp), (3, xm))):
            cp = rcopy(kvout.at[h], kv_all.at[j, ag_rows(d * 2 + rel)],
                       ag_ss.at[h, n], ag_rs.at[j, n, rel], dev(xx, y, z, core))
            cp.start()
            sends.append(cp)

        @pl.when(rel == 1)
        def _():
            rcopy(kvout.at[h], kv_all.at[j, TOK:2 * TOK],
                  ag_ss.at[h, 2], ag_rs.at[j, 2, 1], dev(x, y, z, 1 - c)).start()

        @pl.when(rel == 0)
        def _():
            kv_all[j, 0:TOK] = kvout[h]

    def relay_copy(j, rel, n):
        half = slice(0, HD) if n == 0 else slice(HD, 2 * HD)
        d, xx = ((1, xp), (3, xm))[n]
        return rcopy(kv_all.at[j, (d * 2 + rel) * TOK:(d * 2 + rel + 1) * TOK, half],
                     kv_all.at[j, (4 + rel) * TOK:(5 + rel) * TOK, half],
                     rl_ss.at[j, rel, n], rl_rs.at[j, rel, n], dev(xx, y, z, c))

    def relay(j, rel):
        for n, d in enumerate((1, 3)):
            rcopy(kvout.at[0], kv_all.at[j, (d * 2 + rel) * TOK:(d * 2 + rel + 1) * TOK],
                  ag_ss.at[0, n], ag_rs.at[j, n, rel], dev(xp, y, z, c)).wait_recv()
            cp = relay_copy(j, rel, n)
            cp.start()
            sends.append(cp)

    def gathered(j):
        rcopy(kvout.at[0], kv_all.at[j, TOK:2 * TOK],
              ag_ss.at[0, 2], ag_rs.at[j, 2, 1], dev(x, y, z, 1 - c)).wait_recv()
        for rel in range(2):
            for n in range(2):
                relay_copy(j, rel, n).wait_recv()

    ZR = 2 * ROWS

    def block_rows(b):
        return pl.ds(pl.multiple_of(b * ZR, ZR), ZR)

    def product(j, first, count):
        def one(i, _):
            r = block_rows((z + first + i) % NZ)
            dw[j, r, :] = jnp.dot(xt_all[r, :], kv_all[j], preferred_element_type=F32)
            return 0

        lax.fori_loop(0, count, one, 0)

    def z_copy(j, way, step, sub):
        cols_ = slice(sub * HD, (sub + 1) * HD)
        return rcopy(zsend.at[j, way, step - 1, :, cols_], zrecv.at[j, way, step - 1, :, cols_],
                     z_ss.at[j, way, step - 1, sub], z_rs.at[j, way, step - 1, sub],
                     dev(x, y, zp if way == 0 else zm, c))

    def z_step(j, step):
        for sub in range(2):
            for way in range(2):
                if step == 1 and sub != way:
                    continue
                off = 5 - step if way == 0 else 3 + step
                r = block_rows((z + off) % NZ)
                cols_ = slice(sub * HD, (sub + 1) * HD)
                value = dw[j, r, cols_]
                if step > 2 or (step == 2 and sub == way):
                    z_copy(j, way, step - 1, sub).wait_recv()
                    value = value + zrecv[j, way, step - 2, :, cols_].astype(F32)
                zsend[j, way, step - 1, :, cols_] = value.astype(BF16)
                cp = z_copy(j, way, step, sub)
                cp.start()
                sends.append(cp)

    def y_copy(j, t):
        target = t * 2 + j
        slot = (y - target + 4) % NY - 1
        return rcopy(ysend.at[j, t], yrecv.at[slot], y_ss.at[j, t], y_rs.at[slot],
                     dev(x, target, z, c))

    def z_end(j):
        r = block_rows(z)
        for sub in range(2):
            cols_ = slice(sub * HD, (sub + 1) * HD)
            value = dw[j, r, cols_]
            for way in range(2):
                z_copy(j, way, 4, sub).wait_recv()
                value = value + zrecv[j, way, 3, :, cols_].astype(F32)
            dw[j, r, cols_] = value
            for t in range(2):
                ysend[j, t, :, cols_] = value[t * ROWS:(t + 1) * ROWS].astype(BF16)
        for t in range(2):
            @pl.when(y != t * 2 + j)
            def _(t=t):
                y_copy(j, t).start()

    def y_end(j):
        @pl.when(yl == j)
        def _():
            r = pl.ds(pl.multiple_of(z * ZR + yh * ROWS, ROWS), ROWS)
            total = dw[j, r, :]
            for slot in range(3):
                rcopy(ysend.at[j, 0], yrecv.at[slot], y_ss.at[j, 0], y_rs.at[slot],
                      dev(x, (y + 2) % NY, z, c)).wait_recv()
                total = total + yrecv[slot].astype(F32)
            total = total * (1.0 / 64.0)
            wk_ref[...] = total[:, 0:HD]
            wv_ref[...] = total[:, HD:2 * HD]

    attention(0)
    attention(1)
    finalize(0)
    attention(2)
    finalize(1)
    for d in (1, 3, 2):
        rcopy(xt_send.at[d - 1], xt_slot(xt_all, d, 0), x_ss.at[d - 1], x_rs.at[d - 1],
              dev((x + d) % NX, y, z, c)).wait_recv()
        x_forward(d)
    relay(0, 0)
    relay(0, 1)
    attention(3)
    finalize(2)
    for d in range(4):
        rcopy(xt_slot(xt_all, d, 0), xt_slot(xt_all, d, 1), xf_ss.at[d], xf_rs.at[d],
              dev(x, y, z, 1 - c)).wait_recv()
    gathered(0)
    product(0, 4, 1)
    z_step(0, 1)
    product(0, 5, 7)
    z_step(0, 2)
    finalize(3)
    z_step(0, 3)
    relay(1, 0)
    relay(1, 1)
    z_step(0, 4)
    gathered(1)
    product(1, 4, 1)
    z_step(1, 1)
    product(1, 5, 7)
    z_end(0)
    for step in (2, 3, 4):
        z_step(1, step)
    y_end(0)
    z_end(1)
    y_end(1)

    for cp in sends:
        cp.wait_send()
    for h in range(KVH):
        @pl.when((c + h) % 2 == 1)
        def _(h=h):
            rcopy(kvout.at[h], kv_all.at[h // 2, TOK:2 * TOK],
                  ag_ss.at[h, 2], ag_rs.at[h // 2, 2, 1], dev(x, y, z, 1 - c)).wait_send()
    for j in range(2):
        for t in range(2):
            @pl.when(y != t * 2 + j)
            def _(j=j, t=t):
                y_copy(j, t).wait_send()
    for cp in out_copies:
        cp.wait()


def per_device(layer_input, query_states, key_states, value_states, output_grads, doc_lengths):
    any_spec = pl.BlockSpec(memory_space=pl.ANY)
    vmem = pl.BlockSpec(memory_space=pltpu.VMEM)
    dma = pltpu.SemaphoreType.DMA
    dq, wk, wv = pl.pallas_call(
        kernel,
        out_shape=(
            jax.ShapeDtypeStruct((TOK, KVH * GROUP * HD), BF16),
            jax.ShapeDtypeStruct((ROWS, HD), F32),
            jax.ShapeDtypeStruct((ROWS, HD), F32),
        ),
        in_specs=[pl.BlockSpec(memory_space=pltpu.SMEM)] + [any_spec] * 5,
        out_specs=(any_spec, vmem, vmem),
        scratch_shapes=[
            pltpu.VMEM((TOK, D), BF16),
            pltpu.VMEM((TOK, KVH * GROUP * HD), BF16),
            pltpu.VMEM((TOK, KVH * GROUP * HD), BF16),
            pltpu.VMEM((KVH, 2, 3 * TOK, HD), BF16),
            pltpu.VMEM((TOK, 3 * TOK), F32),
            pltpu.VMEM((GROUP * TOK, 3 * TOK), BF16),
            pltpu.VMEM((GROUP * TOK, 3 * TOK), BF16),
            pltpu.VMEM((TOK, KVH * GROUP * HD), BF16),
            pltpu.VMEM((3, XW, TOK), BF16),
            pltpu.VMEM((XW, 8 * TOK), BF16),
            pltpu.VMEM((KVH, 2, HD, TOK), F32),
            pltpu.VMEM((KVH, 2, 2, HD, TOK), BF16),
            pltpu.VMEM((KVH, 2, 2, HD, TOK), BF16),
            pltpu.VMEM((KVH, TOK, 2 * HD), BF16),
            pltpu.VMEM((2, 8 * TOK, 2 * HD), BF16),
            pltpu.VMEM((2, XW, 2 * HD), F32),
            pltpu.VMEM((2, 2, 4, 2 * ROWS, 2 * HD), BF16),
            pltpu.VMEM((2, 2, 4, 2 * ROWS, 2 * HD), BF16),
            pltpu.VMEM((2, 2, ROWS, 2 * HD), BF16),
            pltpu.VMEM((3, ROWS, 2 * HD), BF16),
            dma((11,)),
            dma((KVH, 2)), dma((KVH, 2)),
            dma((3,)), dma((3,)),
            dma((4,)), dma((4,)),
            dma((KVH, 2)), dma((KVH, 2)),
            dma((KVH, 3)), dma((2, 3, 2)),
            dma((2, 2, 2)), dma((2, 2, 2)),
            dma((2, 2, 4, 2)), dma((2, 2, 4, 2)),
            dma((2, 2)), dma((3,)),
            dma((KVH,)),
        ],
        compiler_params=pltpu.CompilerParams(
            collective_id=0, has_side_effects=True, vmem_limit_bytes=40 * 1024 * 1024,
        ),
        cost_estimate=pl.CostEstimate(
            flops=2_600_000_000, bytes_accessed=4_000_000, transcendentals=1_000_000),
    )(doc_lengths, layer_input[0], query_states[0], key_states[0], value_states[0],
      output_grads[0])
    return dq[None], wk, wv


def solution(mesh):
    return jax.shard_map(
        per_device,
        mesh=mesh,
        in_specs=(
            P("dp", "seq", None),
            P("dp", "seq", None),
            P("dp", "seq", None),
            P("dp", "seq", None),
            P("dp", "seq", None),
            P("dp", None),
        ),
        out_specs=(P("dp", "seq", None), P("dp", "seq"), P("dp", "seq")),
        check_vma=False,
    )
```

```python
import jax
import jax.numpy as jnp
from jax import lax
from jax.experimental import pallas as pl
from jax.experimental.pallas import tpu as pltpu
from jax.sharding import PartitionSpec as P

HD = 128
KVH = 4
GROUP = 5
TOK = 128
D = 5120
XW = D // 4
NX, NY, NZ = 4, 4, 8
ROWS = 80
LOG2E = 1.4426950408889634
SCALE = HD ** (-0.5)
MESH = pl.DeviceIdType.MESH
F32 = jnp.float32
BF16 = jnp.bfloat16


def kernel(
    doc_ref, x_hbm, q_hbm, k_hbm, v_hbm, do_hbm,
    dq_ref, wk_ref, wv_ref,
    xin, qin, doin, kv, bias, ds_s, pb_s, xt_send, xt_all,
    part_own, part_send, part_recv, kvout, kv_all, dw, a_send, a_recv, b_send, b_recv,
    fa_send, fb_send, fa, fb,
    ld_sem, kv_ss, kv_rs, x_ss, x_rs, xl_sem, xf_ss, xf_rs, p_ss, p_rs,
    ag_ss, ag_rs, a_ss, a_rs, b_ss, b_rs, fa_ss, fa_rs, fb_ss, fb_rs,
):
    dp = lax.axis_index("dp")
    sq = lax.axis_index("seq")
    x = dp // 16
    z = (dp // 2) % 8
    yh = dp % 2
    yl = sq // 2
    c = sq % 2
    y = yh * 2 + yl

    def dev(xx, yy, zz, cc):
        return ((xx * 8 + zz) * 2 + yy // 2, (yy % 2) * 2 + cc)

    def seq_dev(delta):
        return (dp, (sq + delta) % 4)

    sibling = dev(x, y, z, 1 - c)

    def rcopy(src, dst, ss, rs, device):
        return pltpu.make_async_remote_copy(
            src_ref=src, dst_ref=dst, send_sem=ss, recv_sem=rs,
            device_id=device, device_id_type=MESH,
        )

    load_x = pltpu.make_async_copy(x_hbm, xin, ld_sem.at[8])
    load_q = pltpu.make_async_copy(q_hbm, qin, ld_sem.at[9])
    load_do = pltpu.make_async_copy(do_hbm, doin, ld_sem.at[10])
    loads = []
    for h in range(KVH):
        for i, ref in enumerate((k_hbm, v_hbm)):
            loads.append(pltpu.make_async_copy(
                ref.at[:, h * HD:(h + 1) * HD], kv.at[h, i, 256:384], ld_sem.at[h * 2 + i]))
    load_x.start()
    for cp in loads:
        cp.start()
    load_q.start()
    load_do.start()

    barrier = pltpu.get_barrier_semaphore()
    out_y = (y + 3 + 2 * yl) % NY
    peers = [dev(x, y, (z + d) % NZ, cc) for d in (4, 3, 5, 2, 6, 1, 7) for cc in (c, 1 - c)]
    peers += [dev((x + d) % NX, y, z, cc) for d in (2, 1, 3) for cc in (c, 1 - c)]
    peers += [dev(x, yy, z, cc) for yy in ((y + 2) % NY, out_y) for cc in (c, 1 - c)]
    peers += [seq_dev(1), seq_dev(2), seq_dev(3)]
    for peer in peers:
        pl.semaphore_signal(barrier, inc=1, device_id=peer, device_id_type=MESH)

    def turn_block(d):
        target = (x + d) % NX

        def turn(i, _):
            col = pl.multiple_of(target * XW + i * 128, 128)
            row = pl.multiple_of(i * 128, 128)
            xt_send[d, pl.ds(row, 128), :] = xin[:, pl.ds(col, 128)].T
            return 0

        lax.fori_loop(0, XW // 128, turn, 0)

    def x_slot(d, rel, t):
        return xt_all.at[t, :, :, (d * 2 + rel) * TOK:(d * 2 + rel + 1) * TOK]

    def x_copy(d, t):
        src = xt_send.at[d].reshape(NZ, 2, ROWS, TOK).at[:, t]
        if d == 0:
            return pltpu.make_async_copy(src, x_slot(0, 0, t), xl_sem.at[t])
        return rcopy(src, x_slot(d, 0, t), x_ss.at[d - 1, t], x_rs.at[d - 1, t],
                     dev((x + d) % NX, y, z, c))

    def x_forward(d, t):
        return rcopy(x_slot(d, 0, t), x_slot(d, 1, t), xf_ss.at[d, t], xf_rs.at[d, t], sibling)

    sends = []

    def start(cp):
        cp.start()
        sends.append(cp)

    load_x.wait()
    turn_block(2)

    for cp in loads:
        cp.wait()
    pl.semaphore_wait(barrier, len(peers))

    def kv_copy(h, delta):
        return rcopy(kv.at[h, :, 256:384], kv.at[h, :, (2 - delta) * TOK:(3 - delta) * TOK],
                     kv_ss.at[h, delta - 1], kv_rs.at[h, delta - 1], seq_dev(delta))

    for h in range(KVH):
        for delta in (2, 1):
            start(kv_copy(h, delta))
    for d in (2, 1, 3, 0):
        if d != 2:
            turn_block(d)
        for t in range(2):
            if d == 0:
                x_copy(0, t).start()
            else:
                start(x_copy(d, t))

    rows = lax.broadcasted_iota(jnp.int32, (TOK, 1), 0) + sq * TOK
    first = jnp.zeros((TOK, 1), jnp.int32)
    end = jnp.int32(0)
    for n in range(6):
        end = end + doc_ref[0, n]
        first = jnp.where(rows >= end, end, first)
    cols = lax.broadcasted_iota(jnp.int32, (TOK, 384), 1) + (sq - 2) * TOK
    bias[...] = jnp.where((cols >= first) & (cols <= rows), 0.0, -1e30).astype(F32)

    load_q.wait()
    load_do.wait()

    def part_copy(h, delta):
        return rcopy(part_send.at[h, delta - 1], part_recv.at[h, delta - 1],
                     p_ss.at[h, delta - 1], p_rs.at[h, delta - 1], seq_dev(4 - delta))

    def attention(h):
        for delta in (1, 2):
            kv_copy(h, delta).wait_recv()
        for g in range(GROUP):
            at = slice((h * GROUP + g) * HD, (h * GROUP + g + 1) * HD)
            to = slice(g * TOK, (g + 1) * TOK)
            kk = kv[h, 0]
            s = lax.dot_general(qin[:, at], kk, (((1,), (1,)), ((), ())),
                                preferred_element_type=F32)
            s = s * (SCALE * LOG2E) + bias[...]
            m = jnp.max(s, axis=1, keepdims=True)
            e = jnp.exp2(s - m)
            p = e * (1.0 / jnp.sum(e, axis=1, keepdims=True))
            dpr = lax.dot_general(doin[:, at], kv[h, 1], (((1,), (1,)), ((), ())),
                                  preferred_element_type=F32)
            delta_r = jnp.sum(p * dpr, axis=1, keepdims=True)
            ds = (p * (dpr - delta_r) * SCALE).astype(BF16)
            ds_s[to, :] = ds
            pb_s[to, :] = p.astype(BF16)
            dq_ref[:, at] = jnp.dot(ds, kk, preferred_element_type=F32).astype(BF16)
        for i, (src, grads) in enumerate(((qin, ds_s), (doin, pb_s))):
            stacked = jnp.concatenate(
                [src[:, (h * GROUP + g) * HD:(h * GROUP + g + 1) * HD] for g in range(GROUP)],
                axis=0)
            t = lax.dot_general(stacked, grads[...], (((0,), (0,)), ((), ())),
                                preferred_element_type=F32)
            part_own[h, i] = t[:, 256:384]
            part_send[h, 0, i] = t[:, 128:256].astype(BF16)
            part_send[h, 1, i] = t[:, 0:128].astype(BF16)
        for delta in (2, 1):
            start(part_copy(h, delta))

    def ag_copy(h, i, d):
        rel = (c + i) % 2
        rows_ = pl.ds(pl.multiple_of((d * 2 + rel) * TOK, TOK), TOK)
        return rcopy(kvout.at[h, i], kv_all.at[h, rows_], ag_ss.at[h, i, d - 1],
                     ag_rs.at[h, d, rel], dev((x + d) % NX, y, z, i))

    def ag_sibling(h):
        return rcopy(kvout.at[h, 1 - c], kv_all.at[h, TOK:2 * TOK],
                     ag_ss.at[h, 0, 3], ag_rs.at[h, 0, 1], sibling)

    def finalize(h):
        for delta in (1, 2):
            part_copy(h, delta).wait_recv()
        for i in range(2):
            total = (part_own[h, i] + part_recv[h, 0, i].astype(F32)
                     + part_recv[h, 1, i].astype(F32))
            kvout[h, i] = total.T.astype(BF16)
        for d in (2, 1, 3):
            for i in range(2):
                start(ag_copy(h, i, d))
        start(ag_sibling(h))
        kv_all[h, 0:TOK] = kvout[h, c]

    def gathered(h):
        ag_sibling(h).wait_recv()
        for d in (1, 3, 2):
            for rel in range(2):
                rcopy(kvout.at[h, 0], kv_all.at[h, (d * 2 + rel) * TOK:(d * 2 + rel + 1) * TOK],
                      ag_ss.at[h, 0, 0], ag_rs.at[h, d, rel], sibling).wait_recv()

    HALF = NZ * ROWS

    def product(h):
        for part in range(2):
            t = c if part == 0 else 1 - c
            for n in range(2):
                w = xt_all[t, n * 4:(n + 1) * 4].reshape(HALF // 2, 8 * TOK)
                out = jnp.dot(w, kv_all[h], preferred_element_type=F32)
                out = out.reshape(4, ROWS, HD)
                dw[h, part, n * 4:(n + 1) * 4] = out
                send = a_send if part == 0 else b_send
                send[h, n * 4:(n + 1) * 4] = out.astype(BF16)
            if part == 0:
                for d in (4, 3, 5, 2, 6, 1, 7):
                    start(a_copy(h, d))
            else:
                @pl.when(y != (1 - c) * 2 + h // 2)
                def _():
                    b_copy(h).start()

    def a_copy(h, d):
        target = (z + d) % NZ
        return rcopy(a_send.at[h, target], a_recv.at[h, d - 1], a_ss.at[h, d - 1],
                     a_rs.at[h, d - 1], dev(x, y, target, c))

    def b_copy(h):
        target = (1 - c) * 2 + h // 2
        slot = (y - target + 4) % NY - 1
        return rcopy(b_send.at[h], b_recv.at[h % 2, slot], b_ss.at[h], b_rs.at[h % 2, slot],
                     dev(x, target, z, c))

    def fa_copy(h):
        return rcopy(fa_send.at[h], fa.at[y], fa_ss.at[h], fa_rs.at[y],
                     dev(x, c * 2 + h // 2, z, h % 2))

    def fa_self(h):
        return (y == c * 2 + h // 2) & (c == h % 2)

    def fb_copy(h, target):
        return rcopy(fb_send.at[h % 2, target], fb.at[z], fb_ss.at[h % 2, target], fb_rs.at[z],
                     dev(x, y, target, h % 2))

    def b_owner(h):
        return y == (1 - c) * 2 + h // 2

    def spread(h):
        for d in range(1, NZ):
            a_copy(h, d).wait_recv()
        total = dw[h, 0, z]
        for d in range(1, NZ):
            total = total + a_recv[h, d - 1].astype(F32)
        total = total.astype(BF16)
        fa_send[h] = total

        @pl.when(fa_self(h))
        def _():
            fa[y] = total

        @pl.when(jnp.logical_not(fa_self(h)))
        def _():
            fa_copy(h).start()

        @pl.when(b_owner(h))
        def _():
            for slot in range(3):
                rcopy(b_send.at[h], b_recv.at[h % 2, slot], b_ss.at[h], b_rs.at[h % 2, slot],
                      dev(x, (y + 2) % NY, z, c)).wait_recv()
            t = dw[h, 1]
            for slot in range(3):
                t = t + b_recv[h % 2, slot].astype(F32)
            fb_send[h % 2] = t.astype(BF16)
            for d in (4, 3, 5, 2, 6, 1, 7):
                fb_copy(h, (z + d) % NZ).start()

            @pl.when(c != h % 2)
            def _():
                fb_copy(h, z).start()

            @pl.when(c == h % 2)
            def _():
                fb[z] = fb_send[h % 2, z]

    def finish():
        own_a = yh == c
        for s in range(NY):
            @pl.when(jnp.logical_not(own_a & (y == s)))
            def _(s=s):
                rcopy(fa_send.at[0], fa.at[s], fa_ss.at[0], fa_rs.at[s], sibling).wait_recv()
        for s in range(NZ):
            @pl.when(own_a | (z != s))
            def _(s=s):
                rcopy(fa_send.at[0], fb.at[s], fa_ss.at[0], fb_rs.at[s], sibling).wait_recv()
        ta = fa[0].astype(F32)
        for s in range(1, NY):
            ta = ta + fa[s].astype(F32)
        tb = fb[0].astype(F32)
        for s in range(1, NZ):
            tb = tb + fb[s].astype(F32)
        ta = ta * (1.0 / 64.0)
        tb = tb * (1.0 / 64.0)
        wk_ref[...] = jnp.where(yh == 0, ta, tb)
        wv_ref[...] = jnp.where(yh == 0, tb, ta)

    attention(0)
    start_x0 = [x_copy(0, t) for t in range(2)]
    for t in range(2):
        start_x0[t].wait()
        start(x_forward(0, t))
    attention(1)
    attention(2)
    finalize(0)
    attention(3)
    finalize(1)
    finalize(2)
    for d in (1, 3, 2):
        for t in range(2):
            x_copy(d, t).wait_recv()
            start(x_forward(d, t))
    finalize(3)
    for d in range(4):
        for t in range(2):
            x_forward(d, t).wait_recv()
    for h in range(KVH):
        gathered(h)
        product(h)
        if h > 0:
            spread(h - 1)
    spread(3)
    finish()

    for cp in sends:
        cp.wait_send()
    for h in range(KVH):
        @pl.when(jnp.logical_not(b_owner(h)))
        def _(h=h):
            b_copy(h).wait_send()

        @pl.when(jnp.logical_not(fa_self(h)))
        def _(h=h):
            fa_copy(h).wait_send()

        @pl.when(b_owner(h))
        def _(h=h):
            for d in range(1, NZ):
                fb_copy(h, (z + d) % NZ).wait_send()

            @pl.when(c != h % 2)
            def _():
                fb_copy(h, z).wait_send()


def per_device(layer_input, query_states, key_states, value_states, output_grads, doc_lengths):
    hbm = pl.BlockSpec(memory_space=pltpu.HBM)
    vmem = pl.BlockSpec(memory_space=pltpu.VMEM)
    dma = pltpu.SemaphoreType.DMA
    dq, wk, wv = pl.pallas_call(
        kernel,
        out_shape=(
            jax.ShapeDtypeStruct((TOK, KVH * GROUP * HD), BF16),
            jax.ShapeDtypeStruct((ROWS, HD), F32),
            jax.ShapeDtypeStruct((ROWS, HD), F32),
        ),
        in_specs=[pl.BlockSpec(memory_space=pltpu.SMEM)] + [hbm] * 5,
        out_specs=(vmem, vmem, vmem),
        scratch_shapes=[
            pltpu.VMEM((TOK, D), BF16),
            pltpu.VMEM((TOK, KVH * GROUP * HD), BF16),
            pltpu.VMEM((TOK, KVH * GROUP * HD), BF16),
            pltpu.VMEM((KVH, 2, 3 * TOK, HD), BF16),
            pltpu.VMEM((TOK, 3 * TOK), F32),
            pltpu.VMEM((GROUP * TOK, 3 * TOK), BF16),
            pltpu.VMEM((GROUP * TOK, 3 * TOK), BF16),
            pltpu.VMEM((4, XW, TOK), BF16),
            pltpu.VMEM((2, NZ, ROWS, 8 * TOK), BF16),
            pltpu.VMEM((KVH, 2, HD, TOK), F32),
            pltpu.VMEM((KVH, 2, 2, HD, TOK), BF16),
            pltpu.VMEM((KVH, 2, 2, HD, TOK), BF16),
            pltpu.VMEM((KVH, 2, TOK, HD), BF16),
            pltpu.VMEM((KVH, 8 * TOK, HD), BF16),
            pltpu.VMEM((KVH, 2, NZ, ROWS, HD), F32),
            pltpu.VMEM((KVH, NZ, ROWS, HD), BF16),
            pltpu.VMEM((KVH, NZ - 1, ROWS, HD), BF16),
            pltpu.VMEM((KVH, NZ, ROWS, HD), BF16),
            pltpu.VMEM((2, 3, NZ, ROWS, HD), BF16),
            pltpu.VMEM((KVH, ROWS, HD), BF16),
            pltpu.VMEM((2, NZ, ROWS, HD), BF16),
            pltpu.VMEM((NY, ROWS, HD), BF16),
            pltpu.VMEM((NZ, ROWS, HD), BF16),
            dma((11,)),
            dma((KVH, 2)), dma((KVH, 2)),
            dma((3, 2)), dma((3, 2)), dma((2,)),
            dma((4, 2)), dma((4, 2)),
            dma((KVH, 2)), dma((KVH, 2)),
            dma((KVH, 2, 4)), dma((KVH, 4, 2)),
            dma((KVH, NZ - 1)), dma((KVH, NZ - 1)),
            dma((KVH,)), dma((2, 3)),
            dma((KVH,)), dma((NY,)),
            dma((2, NZ)), dma((NZ,)),
        ],
        compiler_params=pltpu.CompilerParams(
            collective_id=0, has_side_effects=True, vmem_limit_bytes=40 * 1024 * 1024,
        ),
        cost_estimate=pl.CostEstimate(
            flops=2_600_000_000, bytes_accessed=4_000_000, transcendentals=1_000_000),
    )(pltpu.with_memory_space_constraint(doc_lengths, pltpu.HBM), *[pltpu.with_memory_space_constraint(a[0], pltpu.HBM) for a in (
        layer_input, query_states, key_states, value_states, output_grads)])
    return dq[None], wk, wv


def solution(mesh):
    return jax.shard_map(
        per_device,
        mesh=mesh,
        in_specs=(
            P("dp", "seq", None),
            P("dp", "seq", None),
            P("dp", "seq", None),
            P("dp", "seq", None),
            P("dp", "seq", None),
            P("dp", None),
        ),
        out_specs=(P("dp", "seq", None), P("dp", "seq"), P("dp", "seq")),
        check_vma=False,
    )
```

```python
import jax
import jax.numpy as jnp
from jax import lax
from jax.experimental import pallas as pl
from jax.experimental.pallas import tpu as pltpu
from jax.sharding import PartitionSpec as P

HD = 128
KVH = 4
GROUP = 5
TOK = 128
D = 5120
XW = D // 4
NX, NY, NZ = 4, 4, 8
ROWS = 80
LOG2E = 1.4426950408889634
SCALE = HD ** (-0.5)
MESH = pl.DeviceIdType.MESH
F32 = jnp.float32
BF16 = jnp.bfloat16


def kernel(
    doc_ref, x_hbm, q_hbm, k_hbm, v_hbm, do_hbm,
    dq_ref, wk_ref, wv_ref,
    xin, qin, doin, kv, bias, xt_send, xt_all,
    part_own, part_send, part_recv, kvout, kv_all, a_send, a_recv, b_send, b_recv,
    fa_send, fb_send, fa, fb,
    ld_sem, kv_ss, kv_rs, x_ss, x_rs, xl_sem, xf_ss, xf_rs, p_ss, p_rs,
    ag_ss, ag_rs, a_ss, a_rs, b_ss, b_rs, fa_ss, fa_rs, fb_ss, fb_rs,
):
    dp = lax.axis_index("dp")
    sq = lax.axis_index("seq")
    div, rem = lax.div, lax.rem
    x, z, yh = div(dp, 16), rem(div(dp, 2), 8), rem(dp, 2)
    yl, c = div(sq, 2), rem(sq, 2)
    y = yh * 2 + yl
    xl, xh, zl, zh = rem(x, 2), div(x, 2), rem(z, 2), div(z, 2)
    x_next = (x + 1 - 2 * xl, rem(x + 3 + 2 * xl, NX))
    z_next = (z + 1 - 2 * zl, rem(z + 7 + 2 * zl, NZ))
    x_two = rem(x + 2, NX)
    zh_on = [zh] + [rem(zh + k, 4) for k in (1, 2, 3)]
    z_on = [zl + 2 * k for k in zh_on]
    ranks = [sq] + [rem(sq + k, 4) for k in (1, 2, 3)]
    here, over, across, beyond = (yh, yl), (1 - yh, yl), (yh, 1 - yl), (1 - yh, 1 - yl)

    def member(t, m):
        return (x_next[t] if m // 2 else x), (z_next[t] if m % 2 else z)

    def dev(xx, yy, zz, cc):
        return (xx * 16 + zz * 2 + yy[0], yy[1] * 2 + cc)

    def seq_dev(delta):
        return (dp, ranks[delta])

    sibling = dev(x, here, z, 1 - c)

    def rcopy(src, dst, ss, rs, device):
        return pltpu.make_async_remote_copy(
            src_ref=src, dst_ref=dst, send_sem=ss, recv_sem=rs,
            device_id=device, device_id_type=MESH,
        )

    load_x = pltpu.make_async_copy(x_hbm, xin, ld_sem.at[8])
    load_q = pltpu.make_async_copy(q_hbm, qin, ld_sem.at[9])
    load_do = pltpu.make_async_copy(do_hbm, doin, ld_sem.at[10])
    loads = []
    for h in range(KVH):
        for i, ref in enumerate((k_hbm, v_hbm)):
            loads.append(pltpu.make_async_copy(
                ref.at[:, h * HD:(h + 1) * HD], kv.at[h, i, 256:384], ld_sem.at[h * 2 + i]))
    load_x.start()
    for cp in loads:
        cp.start()
    load_q.start()
    load_do.start()

    barrier = pltpu.get_barrier_semaphore()
    peers = [seq_dev(1), seq_dev(2), seq_dev(3)]
    for t in range(2):
        for m in (3, 2, 1):
            xx, zz = member(t, m)
            peers += [dev(xx, here, zz, c), dev(xx, here, zz, 1 - c)]
    for k in (2, 1, 3, 0):
        zz = z_on[k]
        places = [(x_two, here), (x, over), (x, beyond)]
        if k > 0:
            places += [(x, here), (x, across)]
        for xx, yy in places:
            peers += [dev(xx, yy, zz, c), dev(xx, yy, zz, 1 - c)]
    for peer in peers:
        pl.semaphore_signal(barrier, inc=1, device_id=peer, device_id_type=MESH)

    def turn_block(xd):
        def turn(i, _):
            at = pl.multiple_of(xd * XW + i * 128, 128)
            xt_send[pl.ds(at, 128), :] = xin[:, pl.ds(at, 128)].T
            return 0

        lax.fori_loop(0, XW // 128, turn, 0)

    def x_copy(t, m):
        xx, zz = member(t, m)
        xo, zo = (1 - xl if m // 2 else xl), (1 - zl if m % 2 else zl)
        src = xt_send.reshape(2, 2, 4, 2, 2, ROWS, TOK).at[:, xo, :, zo, t]
        if m == 0:
            return pltpu.make_async_copy(src, xt_all.at[t, 0], xl_sem.at[t])
        return rcopy(src, xt_all.at[t, m * 2], x_ss.at[t, m - 1], x_rs.at[t, m - 1],
                     dev(xx, here, zz, c))

    def x_forward(t, m):
        return rcopy(xt_all.at[t, m * 2], xt_all.at[t, m * 2 + 1], xf_ss.at[t, m], xf_rs.at[t, m],
                     sibling)

    sends = []

    def start(cp):
        cp.start()
        sends.append(cp)

    for cp in loads:
        cp.wait()
    pl.semaphore_wait(barrier, len(peers))

    def kv_copy(h, delta):
        return rcopy(kv.at[h, :, 256:384], kv.at[h, :, (2 - delta) * TOK:(3 - delta) * TOK],
                     kv_ss.at[h, delta - 1], kv_rs.at[h, delta - 1], seq_dev(delta))

    for h in range(KVH):
        for delta in (2, 1):
            @pl.when(sq + delta < 4)
            def _(h=h, delta=delta):
                kv_copy(h, delta).start()
    for delta in (1, 2):
        @pl.when(sq < delta)
        def _(delta=delta):
            kv[:, :, (2 - delta) * TOK:(3 - delta) * TOK] = jnp.zeros((KVH, 2, TOK, HD), BF16)

        @pl.when(sq + delta > 3)
        def _(delta=delta):
            part_recv[:, delta - 1] = jnp.zeros((KVH, 2, HD, TOK), BF16)
    load_x.wait()
    for part in (1, 0):
        for half in range(2):
            turn_block((1 - xl if part else xl) + 2 * half)
        for t in range(2):
            if part:
                start(x_copy(t, 3))
                start(x_copy(t, 2))
            else:
                start(x_copy(t, 1))
                x_copy(t, 0).start()

    rows = lax.broadcasted_iota(jnp.int32, (TOK, 1), 0) + sq * TOK
    first = jnp.zeros((TOK, 1), jnp.int32)
    end = jnp.int32(0)
    for n in range(6):
        end = end + doc_ref[0, n]
        first = jnp.where(rows >= end, end, first)
    cols = lax.broadcasted_iota(jnp.int32, (TOK, 384), 1) + (sq - 2) * TOK
    bias[...] = jnp.where((cols >= first) & (cols <= rows), 0.0, -1e30).astype(F32)

    load_q.wait()
    load_do.wait()

    def part_copy(h, delta):
        return rcopy(part_send.at[h, delta - 1], part_recv.at[h, delta - 1],
                     p_ss.at[h, delta - 1], p_rs.at[h, delta - 1], seq_dev(4 - delta))

    def attention(h):
        for delta in (1, 2):
            @pl.when(sq >= delta)
            def _(delta=delta):
                kv_copy(h, delta).wait_recv()
        def stack(ref):
            return jnp.concatenate(
                [ref[:, (h * GROUP + g) * HD:(h * GROUP + g + 1) * HD] for g in range(GROUP)],
                axis=0)

        qs, dos = stack(qin), stack(doin)
        kk = kv[h, 0]
        nt = (((1,), (1,)), ((), ()))
        s = lax.dot_general(qs, kk, nt, preferred_element_type=F32).reshape(GROUP, TOK, 3 * TOK)
        dpr = lax.dot_general(dos, kv[h, 1], nt, preferred_element_type=F32)
        dpr = dpr.reshape(GROUP, TOK, 3 * TOK)
        s = s * (SCALE * LOG2E) + bias[...][None]
        m = jnp.max(s, axis=2, keepdims=True)
        e = jnp.exp2(s - m)
        p = e * (1.0 / jnp.sum(e, axis=2, keepdims=True))
        delta_r = jnp.sum(p * dpr, axis=2, keepdims=True)
        ds = (p * (dpr - delta_r) * SCALE).astype(BF16).reshape(GROUP * TOK, 3 * TOK)
        pb = p.astype(BF16).reshape(GROUP * TOK, 3 * TOK)
        tn = (((0,), (0,)), ((), ()))
        for i, (rows_in, grads) in enumerate(((qs, ds), (dos, pb))):
            t = lax.dot_general(rows_in, grads, tn, preferred_element_type=F32)
            part_own[h, i] = t[:, 256:384]
            part_send[h, 0, i] = t[:, 128:256].astype(BF16)
            part_send[h, 1, i] = t[:, 0:128].astype(BF16)
        for delta in (2, 1):
            @pl.when(sq >= delta)
            def _(delta=delta):
                part_copy(h, delta).start()
        dq = jnp.dot(ds, kk, preferred_element_type=F32).astype(BF16)
        for g in range(GROUP):
            dq_ref[:, (h * GROUP + g) * HD:(h * GROUP + g + 1) * HD] = dq[g * TOK:(g + 1) * TOK]

    def ag_copy(h, i, t, m):
        rel = 1 - c if i else c
        rows_ = pl.ds(pl.multiple_of((m * 2 + rel) * TOK, TOK), TOK)
        xx, zz = member(t, m)
        return rcopy(kvout.at[h, i], kv_all.at[t, h, rows_], ag_ss.at[h, i, t, m],
                     ag_rs.at[h, t, m, rel], dev(xx, here, zz, i))

    def ag_sibling(h, t):
        return rcopy(kvout.at[h, 1 - c], kv_all.at[t, h, TOK:2 * TOK],
                     ag_ss.at[h, 0, t, 0], ag_rs.at[h, t, 0, 1], sibling)

    def finalize(h):
        for delta in (1, 2):
            @pl.when(sq + delta < 4)
            def _(delta=delta):
                part_copy(h, delta).wait_recv()
        for i in range(2):
            total = (part_own[h, i] + part_recv[h, 0, i].astype(F32)
                     + part_recv[h, 1, i].astype(F32))
            kvout[h, i] = total.T.astype(BF16)
        for m in (3, 2, 1):
            for t in range(2):
                for i in range(2):
                    start(ag_copy(h, i, t, m))
        for t in range(2):
            start(ag_sibling(h, t))
            kv_all[t, h, 0:TOK] = kvout[h, c]

    def gathered(h):
        for t in range(2):
            ag_sibling(h, t).wait_recv()
            for m in (1, 2, 3):
                for rel in range(2):
                    rcopy(kvout.at[h, 0], kv_all.at[t, h, 0:TOK], ag_ss.at[h, 0, 0, 0],
                          ag_rs.at[h, t, m, rel], sibling).wait_recv()

    HALF = 8 * ROWS

    def product(h):
        for part in range(2):
            t = c if part == 0 else 1 - c
            send = a_send if part == 0 else b_send
            for n in range(2):
                w = jnp.concatenate(
                    [xt_all[t, s, n].reshape(4 * ROWS, TOK) for s in range(8)],
                    axis=1)
                out = jnp.dot(w, kv_all[t, h], preferred_element_type=F32)
                send[h, n * 4:(n + 1) * 4] = out.reshape(4, ROWS, HD).astype(BF16)
            if part == 0:
                start(a_copy(h))
            else:
                @pl.when(y != (1 - c) * 2 + h // 2)
                def _():
                    b_copy(h).start()

    def a_copy(h):
        src = a_send.reshape(KVH, 2, 4, ROWS, HD).at[h, 1 - xh]
        return rcopy(src, a_recv.at[h], a_ss.at[h], a_rs.at[h], dev(x_two, here, z, c))

    def b_copy(h):
        target = (1 - c) * 2 + h // 2
        slot = rem(y - target + 4, NY) - 1
        return rcopy(b_send.at[h], b_recv.at[h % 2, slot], b_ss.at[h], b_rs.at[h % 2, slot],
                     dev(x, (1 - c, h // 2), z, c))

    def fa_copy(h, k):
        return rcopy(fa_send.at[h, k], fa.at[y * 4 + zh], fa_ss.at[h, k], fa_rs.at[y * 4 + zh],
                     dev(x, (c, h // 2), zl + 2 * k, h % 2))

    def fa_self(h, k):
        return (y == c * 2 + h // 2) & (c == h % 2) & (zh == k)

    def fb_copy(h, d):
        xo, zo = (1 - xh if d // 4 else xh), zh_on[d % 4]
        q = xo * 4 + zo
        return rcopy(fb_send.at[h % 2, q], fb.at[xh * 4 + zh], fb_ss.at[h % 2, q],
                     fb_rs.at[xh * 4 + zh], dev(xl + 2 * xo, here, zl + 2 * zo, h % 2))

    def b_owner(h):
        return y == (1 - c) * 2 + h // 2

    def spread(h):
        a_copy(h).wait_recv()
        total = a_send[h, pl.ds(xh * 4, 4)].astype(F32) + a_recv[h].astype(F32)
        fa_send[h] = total.astype(BF16)
        for k in range(4):
            @pl.when(fa_self(h, k))
            def _(k=k):
                fa[y * 4 + zh] = fa_send[h, k]

            @pl.when(jnp.logical_not(fa_self(h, k)))
            def _(k=k):
                fa_copy(h, k).start()

        @pl.when(b_owner(h))
        def _():
            for slot in range(3):
                rcopy(b_send.at[h], b_recv.at[h % 2, slot], b_ss.at[h], b_rs.at[h % 2, slot],
                      dev(x, over, z, c)).wait_recv()
            t = b_send[h].astype(F32)
            for slot in range(3):
                t = t + b_recv[h % 2, slot].astype(F32)
            fb_send[h % 2] = t.astype(BF16)
            for d in (6, 5, 7, 4, 2, 1, 3):
                fb_copy(h, d).start()

            @pl.when(c != h % 2)
            def _():
                fb_copy(h, 0).start()

            @pl.when(c == h % 2)
            def _():
                fb[xh * 4 + zh] = fb_send[h % 2, xh * 4 + zh]

    def finish():
        own_a = yh == c
        for s in range(16):
            @pl.when(jnp.logical_not(own_a & (y * 4 + zh == s)))
            def _(s=s):
                rcopy(fb_send.at[0, 0], fa.at[s], fb_ss.at[0, 0], fa_rs.at[s], sibling).wait_recv()
        for s in range(8):
            @pl.when(own_a | (xh * 4 + zh != s))
            def _(s=s):
                rcopy(fb_send.at[0, 0], fb.at[s], fb_ss.at[0, 0], fb_rs.at[s], sibling).wait_recv()
        ta = fa[0].astype(F32)
        for s in range(1, 16):
            ta = ta + fa[s].astype(F32)
        tb = fb[0].astype(F32)
        for s in range(1, 8):
            tb = tb + fb[s].astype(F32)
        ta = ta * (1.0 / 64.0)
        tb = tb * (1.0 / 64.0)
        wk_ref[...] = jnp.where(yh == 0, ta, tb)
        wv_ref[...] = jnp.where(yh == 0, tb, ta)

    attention(0)
    for t in range(2):
        x_copy(t, 0).wait()
        start(x_forward(t, 0))
    attention(1)
    attention(2)
    finalize(0)
    attention(3)
    finalize(1)
    finalize(2)
    for m in (2, 1, 3):
        for t in range(2):
            x_copy(t, m).wait_recv()
            start(x_forward(t, m))
    finalize(3)
    for m in range(4):
        for t in range(2):
            x_forward(t, m).wait_recv()
    for h in range(KVH):
        gathered(h)
        product(h)
        if h > 1:
            spread(h - 2)
    spread(2)
    spread(3)
    finish()

    for cp in sends:
        cp.wait_send()
    for h in range(KVH):
        for delta in (1, 2):
            @pl.when(sq + delta < 4)
            def _(h=h, delta=delta):
                kv_copy(h, delta).wait_send()

            @pl.when(sq >= delta)
            def _(h=h, delta=delta):
                part_copy(h, delta).wait_send()

        @pl.when(jnp.logical_not(b_owner(h)))
        def _(h=h):
            b_copy(h).wait_send()

        for k in range(4):
            @pl.when(jnp.logical_not(fa_self(h, k)))
            def _(h=h, k=k):
                fa_copy(h, k).wait_send()

        @pl.when(b_owner(h))
        def _(h=h):
            for d in range(1, 8):
                fb_copy(h, d).wait_send()

            @pl.when(c != h % 2)
            def _():
                fb_copy(h, 0).wait_send()


def per_device(layer_input, query_states, key_states, value_states, output_grads, doc_lengths):
    hbm = pl.BlockSpec(memory_space=pltpu.HBM)
    vmem = pl.BlockSpec(memory_space=pltpu.VMEM)
    dma = pltpu.SemaphoreType.DMA
    dq, wk, wv = pl.pallas_call(
        kernel,
        out_shape=(
            jax.ShapeDtypeStruct((TOK, KVH * GROUP * HD), BF16),
            jax.ShapeDtypeStruct((ROWS, HD), F32),
            jax.ShapeDtypeStruct((ROWS, HD), F32),
        ),
        in_specs=[pl.BlockSpec(memory_space=pltpu.SMEM)] + [hbm] * 5,
        out_specs=(vmem, vmem, vmem),
        scratch_shapes=[
            pltpu.VMEM((TOK, D), BF16),
            pltpu.VMEM((TOK, KVH * GROUP * HD), BF16),
            pltpu.VMEM((TOK, KVH * GROUP * HD), BF16),
            pltpu.VMEM((KVH, 2, 3 * TOK, HD), BF16),
            pltpu.VMEM((TOK, 3 * TOK), F32),
            pltpu.VMEM((D, TOK), BF16),
            pltpu.VMEM((2, 8, 2, 4, ROWS, TOK), BF16),
            pltpu.VMEM((KVH, 2, HD, TOK), F32),
            pltpu.VMEM((KVH, 2, 2, HD, TOK), BF16),
            pltpu.VMEM((KVH, 2, 2, HD, TOK), BF16),
            pltpu.VMEM((KVH, 2, TOK, HD), BF16),
            pltpu.VMEM((2, KVH, 8 * TOK, HD), BF16),
            pltpu.VMEM((KVH, 8, ROWS, HD), BF16),
            pltpu.VMEM((KVH, 4, ROWS, HD), BF16),
            pltpu.VMEM((KVH, 8, ROWS, HD), BF16),
            pltpu.VMEM((2, 3, 8, ROWS, HD), BF16),
            pltpu.VMEM((KVH, 4, ROWS, HD), BF16),
            pltpu.VMEM((2, 8, ROWS, HD), BF16),
            pltpu.VMEM((16, ROWS, HD), BF16),
            pltpu.VMEM((8, ROWS, HD), BF16),
            dma((11,)),
            dma((KVH, 2)), dma((KVH, 2)),
            dma((2, 3)), dma((2, 3)), dma((2,)),
            dma((2, 4)), dma((2, 4)),
            dma((KVH, 2)), dma((KVH, 2)),
            dma((KVH, 2, 2, 4)), dma((KVH, 2, 4, 2)),
            dma((KVH,)), dma((KVH,)),
            dma((KVH,)), dma((2, 3)),
            dma((KVH, 4)), dma((16,)),
            dma((2, 8)), dma((8,)),
        ],
        compiler_params=pltpu.CompilerParams(
            collective_id=0, has_side_effects=True, vmem_limit_bytes=40 * 1024 * 1024,
        ),
        cost_estimate=pl.CostEstimate(
            flops=2_600_000_000, bytes_accessed=4_000_000, transcendentals=1_000_000),
    )(pltpu.with_memory_space_constraint(doc_lengths, pltpu.HBM), *[pltpu.with_memory_space_constraint(a[0], pltpu.HBM) for a in (
        layer_input, query_states, key_states, value_states, output_grads)])
    return dq[None], wk, wv


def solution(mesh):
    return jax.shard_map(
        per_device,
        mesh=mesh,
        in_specs=(
            P("dp", "seq", None),
            P("dp", "seq", None),
            P("dp", "seq", None),
            P("dp", "seq", None),
            P("dp", "seq", None),
            P("dp", None),
        ),
        out_specs=(P("dp", "seq", None), P("dp", "seq"), P("dp", "seq")),
        check_vma=False,
    )
```

```python
import jax
import jax.numpy as jnp
from jax import lax
from jax.experimental import pallas as pl
from jax.experimental.pallas import tpu as pltpu
from jax.sharding import PartitionSpec as P

HD = 128
KVH = 4
GROUP = 5
TOK = 128
D = 5120
XW = D // 4
NX, NY, NZ = 4, 4, 8
ROWS = 80
LOG2E = 1.4426950408889634
SCALE = HD ** (-0.5)
MESH = pl.DeviceIdType.MESH
F32 = jnp.float32
BF16 = jnp.bfloat16


def kernel(
    doc_ref, x_hbm, q_hbm, k_hbm, v_hbm, do_hbm,
    dq_ref, w_ref,
    xin, qin, doin, kv, bias, xt_send, xt_all,
    part_own, part_send, part_recv, kvout, kv_all, a_send, a_recv, b_send, b_recv,
    fa_send, fb_send, fa, fb,
    ld_sem, kv_ss, kv_rs, x_ss, x_rs, xl_sem, xf_ss, xf_rs, p_ss, p_rs,
    ag_ss, ag_rs, a_ss, a_rs, b_ss, b_rs, fa_ss, fa_rs, fb_ss, fb_rs, met,
):
    dp = lax.axis_index("dp")
    sq = lax.axis_index("seq")
    div, rem = lax.div, lax.rem
    x, z, yh = div(dp, 16), rem(div(dp, 2), 8), rem(dp, 2)
    yl, c = div(sq, 2), rem(sq, 2)
    y = yh * 2 + yl
    xl, v, zl, zh = rem(x, 2), div(x, 2), rem(z, 2), div(z, 2)
    u = xl + v - 2 * xl * v
    pair = (u, v)
    rest_a, rest_b = v + (u - v) * c, u + (v - u) * c
    x_next = (x + 1 - 2 * xl, rem(x + 3 + 2 * xl, NX))
    z_next = (z + 1 - 2 * zl, rem(z + 7 + 2 * zl, NZ))
    x_a = x_next[1] + (x_next[0] - x_next[1]) * c
    x_b = x_next[0] + (x_next[1] - x_next[0]) * c
    zh_on = [zh] + [rem(zh + k, 4) for k in (1, 2, 3)]
    z_on = [zl + 2 * k for k in zh_on]
    ranks = [sq] + [rem(sq + k, 4) for k in (1, 2, 3)]
    here, over, across, beyond = (yh, yl), (1 - yh, yl), (yh, 1 - yl), (1 - yh, 1 - yl)

    def member(t, m):
        return (x_next[t] if m // 2 else x), (z_next[t] if m % 2 else z)

    def dev(xx, yy, zz, cc):
        return (xx * 16 + zz * 2 + yy[0], yy[1] * 2 + cc)

    def seq_dev(delta):
        return (dp, ranks[delta])

    sibling = dev(x, here, z, 1 - c)

    def rcopy(src, dst, ss, rs, device):
        return pltpu.make_async_remote_copy(
            src_ref=src, dst_ref=dst, send_sem=ss, recv_sem=rs,
            device_id=device, device_id_type=MESH,
        )

    load_x = pltpu.make_async_copy(x_hbm, xin, ld_sem.at[8])
    load_q = pltpu.make_async_copy(q_hbm, qin, ld_sem.at[9])
    load_do = pltpu.make_async_copy(do_hbm, doin, ld_sem.at[10])
    loads = []
    for h in range(KVH):
        for i, ref in enumerate((k_hbm, v_hbm)):
            loads.append(pltpu.make_async_copy(
                ref.at[:, h * HD:(h + 1) * HD], kv.at[h, i, 256:384], ld_sem.at[h * 2 + i]))
    load_x.start()
    for cp in loads:
        cp.start()
    load_q.start()
    load_do.start()

    barrier = pltpu.get_barrier_semaphore()
    peers = [seq_dev(1), seq_dev(2), seq_dev(3)]
    for t in range(2):
        for m in (3, 2, 1):
            xx, zz = member(t, m)
            peers += [dev(xx, here, zz, c), dev(xx, here, zz, 1 - c)]
    for k in (2, 1, 3, 0):
        zz = z_on[k]
        places = [(x, over), (x, beyond)]
        if k > 0:
            places = [(x, here)]
        for xx, yy in places:
            peers += [dev(xx, yy, zz, c), dev(xx, yy, zz, 1 - c)]
    for peer in peers:
        pl.semaphore_signal(barrier, inc=1, device_id=peer, device_id_type=MESH)

    def turn_block(ud, vd):
        def turn(i, _):
            to = pl.multiple_of((2 * ud + vd) * XW + i * 128, 128)
            at = pl.multiple_of((2 * vd + ud + vd - 2 * ud * vd) * XW + i * 128, 128)
            xt_send[pl.ds(to, 128), :] = xin[:, pl.ds(at, 128)].T
            return 0

        lax.fori_loop(0, XW // 128, turn, 0)

    def x_copy(t, m):
        xx, zz = member(t, m)
        xo, zo = (1 - pair[t] if m // 2 else pair[t]), (1 - zl if m % 2 else zl)
        view = xt_send.reshape(2, 2, 4, 2, 2, ROWS, TOK)
        src = view.at[:, xo, :, zo, t] if t else view.at[xo, :, :, zo, t]
        if m == 0:
            return pltpu.make_async_copy(src, xt_all.at[t, 0], xl_sem.at[t])
        return rcopy(src, xt_all.at[t, m * 2], x_ss.at[t, m - 1], x_rs.at[t, m - 1],
                     dev(xx, here, zz, c))

    def x_forward(t, m):
        return rcopy(xt_all.at[t, m * 2], xt_all.at[t, m * 2 + 1], xf_ss.at[t, m], xf_rs.at[t, m],
                     sibling)

    sends = []

    def start(cp):
        cp.start()
        sends.append(cp)

    for cp in loads:
        cp.wait()
    pl.semaphore_wait(barrier, len(peers))

    def kv_copy(h, delta):
        return rcopy(kv.at[h, :, 256:384], kv.at[h, :, (2 - delta) * TOK:(3 - delta) * TOK],
                     kv_ss.at[h, delta - 1], kv_rs.at[h, delta - 1], seq_dev(delta))

    for h in range(KVH):
        for delta in (2, 1):
            @pl.when(sq + delta < 4)
            def _(h=h, delta=delta):
                kv_copy(h, delta).start()
    for xx, yy in ((x, over), (x, beyond), (x, across), (x_next[0], here), (x_next[1], here)):
        pl.semaphore_signal(met, inc=1, device_id=dev(xx, yy, z, c), device_id_type=MESH)
    for delta in (1, 2):
        @pl.when(sq < delta)
        def _(delta=delta):
            kv[:, :, (2 - delta) * TOK:(3 - delta) * TOK] = jnp.zeros((KVH, 2, TOK, HD), BF16)

        @pl.when(sq + delta > 3)
        def _(delta=delta):
            part_recv[:, delta - 1] = jnp.zeros((KVH, 2, HD, TOK), BF16)
    load_x.wait()
    turn_block(1 - u, v)
    turn_block(1 - u, 1 - v)
    start(x_copy(0, 3))
    start(x_copy(0, 2))
    turn_block(u, 1 - v)
    start(x_copy(1, 3))
    start(x_copy(1, 2))
    turn_block(u, v)
    for t in range(2):
        start(x_copy(t, 1))
        x_copy(t, 0).start()

    rows = lax.broadcasted_iota(jnp.int32, (TOK, 1), 0) + sq * TOK
    first = jnp.zeros((TOK, 1), jnp.int32)
    end = jnp.int32(0)
    for n in range(6):
        end = end + doc_ref[0, n]
        first = jnp.where(rows >= end, end, first)
    cols = lax.broadcasted_iota(jnp.int32, (TOK, 384), 1) + (sq - 2) * TOK
    bias[...] = jnp.where((cols >= first) & (cols <= rows), 0.0, -1e30).astype(F32)

    load_q.wait()
    load_do.wait()

    def part_copy(h, delta):
        return rcopy(part_send.at[h, delta - 1], part_recv.at[h, delta - 1],
                     p_ss.at[h, delta - 1], p_rs.at[h, delta - 1], seq_dev(4 - delta))

    def attention(h):
        for delta in (1, 2):
            @pl.when(sq >= delta)
            def _(delta=delta):
                kv_copy(h, delta).wait_recv()
        def stack(ref):
            return jnp.concatenate(
                [ref[:, (h * GROUP + g) * HD:(h * GROUP + g + 1) * HD] for g in range(GROUP)],
                axis=0)

        qs, dos = stack(qin), stack(doin)
        kk = kv[h, 0]
        nt = (((1,), (1,)), ((), ()))
        s = lax.dot_general(qs, kk, nt, preferred_element_type=F32).reshape(GROUP, TOK, 3 * TOK)
        dpr = lax.dot_general(dos, kv[h, 1], nt, preferred_element_type=F32)
        dpr = dpr.reshape(GROUP, TOK, 3 * TOK)
        s = s * (SCALE * LOG2E) + bias[...][None]
        m = jnp.max(s, axis=2, keepdims=True)
        e = jnp.exp2(s - m)
        p = e * (1.0 / jnp.sum(e, axis=2, keepdims=True))
        delta_r = jnp.sum(p * dpr, axis=2, keepdims=True)
        ds = (p * (dpr - delta_r) * SCALE).astype(BF16).reshape(GROUP * TOK, 3 * TOK)
        pb = p.astype(BF16).reshape(GROUP * TOK, 3 * TOK)
        tn = (((0,), (0,)), ((), ()))
        for i, (rows_in, grads) in enumerate(((qs, ds), (dos, pb))):
            t = lax.dot_general(rows_in, grads, tn, preferred_element_type=F32)
            part_own[h, i] = t[:, 256:384]
            part_send[h, 0, i] = t[:, 128:256].astype(BF16)
            part_send[h, 1, i] = t[:, 0:128].astype(BF16)
        for delta in (2, 1):
            @pl.when(sq >= delta)
            def _(delta=delta):
                part_copy(h, delta).start()
        dq = jnp.dot(ds, kk, preferred_element_type=F32).astype(BF16)
        for g in range(GROUP):
            dq_ref[:, (h * GROUP + g) * HD:(h * GROUP + g + 1) * HD] = dq[g * TOK:(g + 1) * TOK]

    def ag_copy(h, i, t, m):
        rel = 1 - c if i else c
        rows_ = pl.ds(pl.multiple_of((m * 2 + rel) * TOK, TOK), TOK)
        xx, zz = member(t, m)
        return rcopy(kvout.at[h, i], kv_all.at[t, h, rows_], ag_ss.at[h, i, t, m],
                     ag_rs.at[h, t, m, rel], dev(xx, here, zz, i))

    def ag_sibling(h, t):
        return rcopy(kvout.at[h, 1 - c], kv_all.at[t, h, TOK:2 * TOK],
                     ag_ss.at[h, 0, t, 0], ag_rs.at[h, t, 0, 1], sibling)

    def finalize(h):
        for delta in (1, 2):
            @pl.when(sq + delta < 4)
            def _(delta=delta):
                part_copy(h, delta).wait_recv()
        for i in range(2):
            total = (part_own[h, i] + part_recv[h, 0, i].astype(F32)
                     + part_recv[h, 1, i].astype(F32))
            kvout[h, i] = total.T.astype(BF16)
        for m in (3, 2, 1):
            for t in range(2):
                for i in range(2):
                    start(ag_copy(h, i, t, m))
        for t in range(2):
            start(ag_sibling(h, t))
            kv_all[t, h, 0:TOK] = kvout[h, c]

    def gathered(h):
        for t in range(2):
            ag_sibling(h, t).wait_recv()
            for m in (1, 2, 3):
                for rel in range(2):
                    rcopy(kvout.at[h, 0], kv_all.at[t, h, 0:TOK], ag_ss.at[h, 0, 0, 0],
                          ag_rs.at[h, t, m, rel], sibling).wait_recv()

    HALF = 8 * ROWS

    def product(h):
        for part in range(2):
            t = c if part == 0 else 1 - c
            send = a_send if part == 0 else b_send
            for n in range(2):
                w = jnp.concatenate(
                    [xt_all[t, s, n].reshape(4 * ROWS, TOK) for s in range(8)],
                    axis=1)
                out = jnp.dot(w, kv_all[t, h], preferred_element_type=F32)
                send[h, n * 4:(n + 1) * 4] = out.reshape(4, ROWS, HD).astype(BF16)
            if part == 0:
                start(a_copy(h))
            else:
                @pl.when(y != (1 - c) * 2 + h // 2)
                def _():
                    b_copy(h).start()

    def a_copy(h):
        src = a_send.reshape(KVH, 2, 4, ROWS, HD).at[h, 1 - rest_a]
        return rcopy(src, a_recv.at[h], a_ss.at[h], a_rs.at[h], dev(x_a, here, z, c))

    def b_copy(h):
        target = (1 - c) * 2 + h // 2
        slot = rem(y - target + 4, NY) - 1
        return rcopy(b_send.at[h], b_recv.at[h % 2, slot], b_ss.at[h], b_rs.at[h % 2, slot],
                     dev(x, (1 - c, h // 2), z, c))

    def fa_copy(h, k):
        return rcopy(fa_send.at[h, k], fa.at[y * 4 + zh], fa_ss.at[h, k], fa_rs.at[y * 4 + zh],
                     dev(x, (c, h // 2), zl + 2 * k, h % 2))

    def fa_self(h, k):
        return (y == c * 2 + h // 2) & (c == h % 2) & (zh == k)

    def fb_copy(h, d):
        xo, zo = (1 - rest_b if d // 4 else rest_b), zh_on[d % 4]
        q = xo * 4 + zo
        return rcopy(fb_send.at[h % 2, q], fb.at[rest_b * 4 + zh], fb_ss.at[h % 2, q],
                     fb_rs.at[rest_b * 4 + zh],
                     dev(x_b if d // 4 else x, here, zl + 2 * zo, h % 2))

    def b_owner(h):
        return y == (1 - c) * 2 + h // 2

    def spread(h):
        a_copy(h).wait_recv()
        total = a_send[h, pl.ds(rest_a * 4, 4)].astype(F32) + a_recv[h].astype(F32)
        fa_send[h] = total.astype(BF16)
        for k in range(4):
            @pl.when(fa_self(h, k))
            def _(k=k):
                fa[y * 4 + zh] = fa_send[h, k]

            @pl.when(jnp.logical_not(fa_self(h, k)))
            def _(k=k):
                fa_copy(h, k).start()

        @pl.when(b_owner(h))
        def _():
            for slot in range(3):
                rcopy(b_send.at[h], b_recv.at[h % 2, slot], b_ss.at[h], b_rs.at[h % 2, slot],
                      dev(x, over, z, c)).wait_recv()
            t = b_send[h].astype(F32)
            for slot in range(3):
                t = t + b_recv[h % 2, slot].astype(F32)
            fb_send[h % 2] = t.astype(BF16)
            for d in (6, 5, 7, 4, 2, 1, 3):
                fb_copy(h, d).start()

            @pl.when(c != h % 2)
            def _():
                fb_copy(h, 0).start()

            @pl.when(c == h % 2)
            def _():
                fb[rest_b * 4 + zh] = fb_send[h % 2, rest_b * 4 + zh]

    def finish():
        own_a = yh == c
        for s in range(16):
            @pl.when(jnp.logical_not(own_a & (y * 4 + zh == s)))
            def _(s=s):
                rcopy(fb_send.at[0, 0], fa.at[s], fb_ss.at[0, 0], fa_rs.at[s], sibling).wait_recv()
        for s in range(8):
            @pl.when(own_a | (rest_b * 4 + zh != s))
            def _(s=s):
                rcopy(fb_send.at[0, 0], fb.at[s], fb_ss.at[0, 0], fb_rs.at[s], sibling).wait_recv()
        ta = fa[0].astype(F32)
        for s in range(1, 16):
            ta = ta + fa[s].astype(F32)
        tb = fb[0].astype(F32)
        for s in range(1, 8):
            tb = tb + fb[s].astype(F32)
        ta = ta * (1.0 / 64.0)
        tb = tb * (1.0 / 64.0)
        w_ref[0] = jnp.where(yh == 0, ta, tb)
        w_ref[1] = jnp.where(yh == 0, tb, ta)

    attention(0)
    for t in range(2):
        x_copy(t, 0).wait()
        start(x_forward(t, 0))
    attention(1)
    attention(2)
    finalize(0)
    attention(3)
    finalize(1)
    finalize(2)
    for m in (2, 1, 3):
        for t in range(2):
            x_copy(t, m).wait_recv()
            start(x_forward(t, m))
    finalize(3)
    for m in range(4):
        for t in range(2):
            x_forward(t, m).wait_recv()
    pl.semaphore_wait(met, 5)
    for h in range(KVH):
        gathered(h)
        product(h)
        if h > 1:
            spread(h - 2)
    spread(2)
    spread(3)
    for cp in sends:
        cp.wait_send()
    for h in range(KVH):
        for delta in (1, 2):
            @pl.when(sq + delta < 4)
            def _(h=h, delta=delta):
                kv_copy(h, delta).wait_send()

            @pl.when(sq >= delta)
            def _(h=h, delta=delta):
                part_copy(h, delta).wait_send()

        @pl.when(jnp.logical_not(b_owner(h)))
        def _(h=h):
            b_copy(h).wait_send()

        for k in range(4):
            @pl.when(jnp.logical_not(fa_self(h, k)))
            def _(h=h, k=k):
                fa_copy(h, k).wait_send()

        @pl.when(b_owner(h))
        def _(h=h):
            for d in range(1, 8):
                fb_copy(h, d).wait_send()

            @pl.when(c != h % 2)
            def _():
                fb_copy(h, 0).wait_send()
    finish()


def per_device(layer_input, query_states, key_states, value_states, output_grads, doc_lengths):
    hbm = pl.BlockSpec(memory_space=pltpu.HBM)
    vmem = pl.BlockSpec(memory_space=pltpu.VMEM)
    dma = pltpu.SemaphoreType.DMA
    dq, w = pl.pallas_call(
        kernel,
        out_shape=(
            jax.ShapeDtypeStruct((TOK, KVH * GROUP * HD), BF16),
            jax.ShapeDtypeStruct((2, ROWS, HD), F32),
        ),
        in_specs=[pl.BlockSpec(memory_space=pltpu.SMEM)] + [hbm] * 5,
        out_specs=(vmem, vmem),
        scratch_shapes=[
            pltpu.VMEM((TOK, D), BF16),
            pltpu.VMEM((TOK, KVH * GROUP * HD), BF16),
            pltpu.VMEM((TOK, KVH * GROUP * HD), BF16),
            pltpu.VMEM((KVH, 2, 3 * TOK, HD), BF16),
            pltpu.VMEM((TOK, 3 * TOK), F32),
            pltpu.VMEM((D, TOK), BF16),
            pltpu.VMEM((2, 8, 2, 4, ROWS, TOK), BF16),
            pltpu.VMEM((KVH, 2, HD, TOK), F32),
            pltpu.VMEM((KVH, 2, 2, HD, TOK), BF16),
            pltpu.VMEM((KVH, 2, 2, HD, TOK), BF16),
            pltpu.VMEM((KVH, 2, TOK, HD), BF16),
            pltpu.VMEM((2, KVH, 8 * TOK, HD), BF16),
            pltpu.VMEM((KVH, 8, ROWS, HD), BF16),
            pltpu.VMEM((KVH, 4, ROWS, HD), BF16),
            pltpu.VMEM((KVH, 8, ROWS, HD), BF16),
            pltpu.VMEM((2, 3, 8, ROWS, HD), BF16),
            pltpu.VMEM((KVH, 4, ROWS, HD), BF16),
            pltpu.VMEM((2, 8, ROWS, HD), BF16),
            pltpu.VMEM((16, ROWS, HD), BF16),
            pltpu.VMEM((8, ROWS, HD), BF16),
            dma((11,)),
            dma((KVH, 2)), dma((KVH, 2)),
            dma((2, 3)), dma((2, 3)), dma((2,)),
            dma((2, 4)), dma((2, 4)),
            dma((KVH, 2)), dma((KVH, 2)),
            dma((KVH, 2, 2, 4)), dma((KVH, 2, 4, 2)),
            dma((KVH,)), dma((KVH,)),
            dma((KVH,)), dma((2, 3)),
            dma((KVH, 4)), dma((16,)),
            dma((2, 8)), dma((8,)),
            pltpu.SemaphoreType.REGULAR,
        ],
        compiler_params=pltpu.CompilerParams(
            collective_id=0, has_side_effects=True, vmem_limit_bytes=40 * 1024 * 1024,
        ),
        cost_estimate=pl.CostEstimate(
            flops=2_600_000_000, bytes_accessed=4_000_000, transcendentals=1_000_000),
    )(pltpu.with_memory_space_constraint(doc_lengths, pltpu.HBM), *[pltpu.with_memory_space_constraint(a[0], pltpu.HBM) for a in (
        layer_input, query_states, key_states, value_states, output_grads)])
    return dq[None], w[0], w[1]


def solution(mesh):
    return jax.shard_map(
        per_device,
        mesh=mesh,
        in_specs=(
            P("dp", "seq", None),
            P("dp", "seq", None),
            P("dp", "seq", None),
            P("dp", "seq", None),
            P("dp", "seq", None),
            P("dp", None),
        ),
        out_specs=(P("dp", "seq", None), P("dp", "seq"), P("dp", "seq")),
        check_vma=False,
    )
```

```python
import jax
import jax.numpy as jnp
from jax import lax
from jax.experimental import pallas as pl
from jax.experimental.pallas import tpu as pltpu
from jax.sharding import PartitionSpec as P

HD = 128
KVH = 4
GROUP = 5
TOK = 128
D = 5120
XW = D // 4
NX, NY, NZ = 4, 4, 8
ORDER = (1, 2, 0, 3)
ROWS = 80
LOG2E = 1.4426950408889634
SCALE = HD ** (-0.5)
MESH = pl.DeviceIdType.MESH
F32 = jnp.float32
BF16 = jnp.bfloat16


def kernel(
    doc_ref, x_hbm, q_hbm, k_hbm, v_hbm, do_hbm,
    dq_ref, w_ref,
    xin, qin, doin, kv, bias, xt_send, xt_all,
    part_own, part_send, part_recv, kvout, kv_all, a_send, a_recv, b_send, b_recv,
    fa_send, fb_send, fa, fb,
    ld_sem, kv_ss, kv_rs, x_ss, x_rs, xl_sem, xf_ss, xf_rs, p_ss, p_rs,
    ag_ss, ag_rs, a_ss, a_rs, b_ss, b_rs, fa_ss, fa_rs, fb_ss, fb_rs, met,
):
    dp = lax.axis_index("dp")
    sq = lax.axis_index("seq")
    div, rem = lax.div, lax.rem
    x, z, yh = div(dp, 16), rem(div(dp, 2), 8), rem(dp, 2)
    yl, c = div(sq, 2), rem(sq, 2)
    y = yh * 2 + yl
    xl, v, zl, zh = rem(x, 2), div(x, 2), rem(z, 2), div(z, 2)
    u = xl + v - 2 * xl * v
    pair = (u, v)
    rest_a, rest_b = v + (u - v) * c, u + (v - u) * c
    x_next = (x + 1 - 2 * xl, rem(x + 3 + 2 * xl, NX))
    z_next = (z + 1 - 2 * zl, rem(z + 7 + 2 * zl, NZ))
    x_a = x_next[1] + (x_next[0] - x_next[1]) * c
    x_b = x_next[0] + (x_next[1] - x_next[0]) * c
    zh_on = [zh] + [rem(zh + k, 4) for k in (1, 2, 3)]
    z_on = [zl + 2 * k for k in zh_on]
    ranks = [sq] + [rem(sq + k, 4) for k in (1, 2, 3)]
    here, over, across, beyond = (yh, yl), (1 - yh, yl), (yh, 1 - yl), (1 - yh, 1 - yl)

    def member(t, m):
        return (x_next[t] if m // 2 else x), (z_next[t] if m % 2 else z)

    def dev(xx, yy, zz, cc):
        return (xx * 16 + zz * 2 + yy[0], yy[1] * 2 + cc)

    def seq_dev(delta):
        return (dp, ranks[delta])

    sibling = dev(x, here, z, 1 - c)

    def rcopy(src, dst, ss, rs, device):
        return pltpu.make_async_remote_copy(
            src_ref=src, dst_ref=dst, send_sem=ss, recv_sem=rs,
            device_id=device, device_id_type=MESH,
        )

    load_x = pltpu.make_async_copy(x_hbm, xin, ld_sem.at[8])
    load_q = pltpu.make_async_copy(q_hbm, qin, ld_sem.at[9])
    load_do = pltpu.make_async_copy(do_hbm, doin, ld_sem.at[10])
    loads = []
    for h in range(KVH):
        for i, ref in enumerate((k_hbm, v_hbm)):
            loads.append(pltpu.make_async_copy(
                ref.at[:, h * HD:(h + 1) * HD], kv.at[h, i, 256:384], ld_sem.at[h * 2 + i]))
    load_x.start()
    for cp in loads:
        cp.start()
    load_q.start()
    load_do.start()

    barrier = pltpu.get_barrier_semaphore()
    peers = [seq_dev(1), seq_dev(2), seq_dev(3)]
    for t in range(2):
        for m in (3, 2, 1):
            xx, zz = member(t, m)
            peers += [dev(xx, here, zz, c), dev(xx, here, zz, 1 - c)]
    for k in (2, 1, 3, 0):
        zz = z_on[k]
        places = [(x, over), (x, beyond)]
        if k > 0:
            places = [(x, here)]
        for xx, yy in places:
            peers += [dev(xx, yy, zz, c), dev(xx, yy, zz, 1 - c)]
    for peer in peers:
        pl.semaphore_signal(barrier, inc=1, device_id=peer, device_id_type=MESH)

    def turn_block(ud, vd):
        def turn(i, _):
            to = pl.multiple_of((2 * ud + vd) * XW + i * 128, 128)
            at = pl.multiple_of((2 * vd + ud + vd - 2 * ud * vd) * XW + i * 128, 128)
            xt_send[pl.ds(to, 128), :] = xin[:, pl.ds(at, 128)].T
            return 0

        lax.fori_loop(0, XW // 128, turn, 0)

    def x_copy(t, m):
        xx, zz = member(t, m)
        xo, zo = (1 - pair[t] if m // 2 else pair[t]), (1 - zl if m % 2 else zl)
        view = xt_send.reshape(2, 2, 4, 2, 2, ROWS, TOK)
        src = view.at[:, xo, :, zo, t] if t else view.at[xo, :, :, zo, t]
        if m == 0:
            return pltpu.make_async_copy(src, xt_all.at[t, 0], xl_sem.at[t])
        return rcopy(src, xt_all.at[t, m * 2], x_ss.at[t, m - 1], x_rs.at[t, m - 1],
                     dev(xx, here, zz, c))

    def x_forward(t, m):
        return rcopy(xt_all.at[t, m * 2], xt_all.at[t, m * 2 + 1], xf_ss.at[t, m], xf_rs.at[t, m],
                     sibling)

    sends = []

    def start(cp):
        cp.start()
        sends.append(cp)

    for cp in loads:
        cp.wait()
    pl.semaphore_wait(barrier, len(peers))

    def kv_copy(h, delta):
        return rcopy(kv.at[h, :, 256:384], kv.at[h, :, (2 - delta) * TOK:(3 - delta) * TOK],
                     kv_ss.at[h, delta - 1], kv_rs.at[h, delta - 1], seq_dev(delta))

    for h in ORDER:
        for delta in (2, 1):
            @pl.when(sq + delta < 4)
            def _(h=h, delta=delta):
                kv_copy(h, delta).start()
    for xx, yy in ((x, over), (x, beyond), (x, across), (x_next[0], here), (x_next[1], here)):
        pl.semaphore_signal(met, inc=1, device_id=dev(xx, yy, z, c), device_id_type=MESH)
    for delta in (1, 2):
        @pl.when(sq < delta)
        def _(delta=delta):
            kv[:, :, (2 - delta) * TOK:(3 - delta) * TOK] = jnp.zeros((KVH, 2, TOK, HD), BF16)

        @pl.when(sq + delta > 3)
        def _(delta=delta):
            part_recv[:, delta - 1] = jnp.zeros((KVH, 2, HD, TOK), BF16)
    load_x.wait()
    turn_block(1 - u, v)
    turn_block(1 - u, 1 - v)
    start(x_copy(0, 3))
    start(x_copy(0, 2))
    turn_block(u, 1 - v)
    start(x_copy(1, 3))
    start(x_copy(1, 2))
    turn_block(u, v)
    for t in range(2):
        start(x_copy(t, 1))
        x_copy(t, 0).start()

    rows = lax.broadcasted_iota(jnp.int32, (TOK, 1), 0) + sq * TOK
    first = jnp.zeros((TOK, 1), jnp.int32)
    end = jnp.int32(0)
    for n in range(6):
        end = end + doc_ref[0, n]
        first = jnp.where(rows >= end, end, first)
    cols = lax.broadcasted_iota(jnp.int32, (TOK, 384), 1) + (sq - 2) * TOK
    bias[...] = jnp.where((cols >= first) & (cols <= rows), 0.0, -1e30).astype(F32)

    load_q.wait()
    load_do.wait()

    def part_copy(h, delta):
        return rcopy(part_send.at[h, delta - 1], part_recv.at[h, delta - 1],
                     p_ss.at[h, delta - 1], p_rs.at[h, delta - 1], seq_dev(4 - delta))

    def attention(h):
        for delta in (1, 2):
            @pl.when(sq >= delta)
            def _(delta=delta):
                kv_copy(h, delta).wait_recv()
        def stack(ref):
            return jnp.concatenate(
                [ref[:, (h * GROUP + g) * HD:(h * GROUP + g + 1) * HD] for g in range(GROUP)],
                axis=0)

        qs, dos = stack(qin), stack(doin)
        kk = kv[h, 0]
        nt = (((1,), (1,)), ((), ()))
        s = lax.dot_general(qs, kk, nt, preferred_element_type=F32).reshape(GROUP, TOK, 3 * TOK)
        dpr = lax.dot_general(dos, kv[h, 1], nt, preferred_element_type=F32)
        dpr = dpr.reshape(GROUP, TOK, 3 * TOK)
        s = s * (SCALE * LOG2E) + bias[...][None]
        m = jnp.max(s, axis=2, keepdims=True)
        e = jnp.exp2(s - m)
        p = e * (1.0 / jnp.sum(e, axis=2, keepdims=True))
        delta_r = jnp.sum(p * dpr, axis=2, keepdims=True)
        ds = (p * (dpr - delta_r) * SCALE).astype(BF16).reshape(GROUP * TOK, 3 * TOK)
        pb = p.astype(BF16).reshape(GROUP * TOK, 3 * TOK)
        tn = (((0,), (0,)), ((), ()))
        for i, (rows_in, grads) in enumerate(((qs, ds), (dos, pb))):
            t = lax.dot_general(rows_in, grads, tn, preferred_element_type=F32)
            part_own[h, i] = t[:, 256:384]
            part_send[h, 0, i] = t[:, 128:256].astype(BF16)
            part_send[h, 1, i] = t[:, 0:128].astype(BF16)
        for delta in (2, 1):
            @pl.when(sq >= delta)
            def _(delta=delta):
                part_copy(h, delta).start()
        dq = jnp.dot(ds, kk, preferred_element_type=F32).astype(BF16)
        for g in range(GROUP):
            dq_ref[:, (h * GROUP + g) * HD:(h * GROUP + g + 1) * HD] = dq[g * TOK:(g + 1) * TOK]

    def ag_copy(h, i, t, m):
        rel = 1 - c if i else c
        rows_ = pl.ds(pl.multiple_of((m * 2 + rel) * TOK, TOK), TOK)
        xx, zz = member(t, m)
        return rcopy(kvout.at[h, i], kv_all.at[t, h, rows_], ag_ss.at[h, i, t, m],
                     ag_rs.at[h, t, m, rel], dev(xx, here, zz, i))

    def ag_sibling(h, t):
        return rcopy(kvout.at[h, 1 - c], kv_all.at[t, h, TOK:2 * TOK],
                     ag_ss.at[h, 0, t, 0], ag_rs.at[h, t, 0, 1], sibling)

    def finalize(h):
        for delta in (1, 2):
            @pl.when(sq + delta < 4)
            def _(delta=delta):
                part_copy(h, delta).wait_recv()
        for i in range(2):
            total = (part_own[h, i] + part_recv[h, 0, i].astype(F32)
                     + part_recv[h, 1, i].astype(F32))
            kvout[h, i] = total.T.astype(BF16)
        for m in (3, 2, 1):
            for t in range(2):
                for i in range(2):
                    start(ag_copy(h, i, t, m))
        for t in range(2):
            start(ag_sibling(h, t))
            kv_all[t, h, 0:TOK] = kvout[h, c]

    def gathered(h):
        for t in range(2):
            ag_sibling(h, t).wait_recv()
            for m in (1, 2, 3):
                for rel in range(2):
                    rcopy(kvout.at[h, 0], kv_all.at[t, h, 0:TOK], ag_ss.at[h, 0, 0, 0],
                          ag_rs.at[h, t, m, rel], sibling).wait_recv()

    HALF = 8 * ROWS

    def product(h):
        for part in range(2):
            t = c if part == 0 else 1 - c
            send = a_send if part == 0 else b_send
            for n in range(2):
                w = jnp.concatenate(
                    [xt_all[t, s, n].reshape(4 * ROWS, TOK) for s in range(8)],
                    axis=1)
                out = jnp.dot(w, kv_all[t, h], preferred_element_type=F32)
                send[h, n * 4:(n + 1) * 4] = out.reshape(4, ROWS, HD).astype(BF16)
            if part == 0:
                start(a_copy(h))
            else:
                @pl.when(y != (1 - c) * 2 + h // 2)
                def _():
                    b_copy(h).start()

    def a_copy(h):
        src = a_send.reshape(KVH, 2, 4, ROWS, HD).at[h, 1 - rest_a]
        return rcopy(src, a_recv.at[h], a_ss.at[h], a_rs.at[h], dev(x_a, here, z, c))

    def b_copy(h):
        target = (1 - c) * 2 + h // 2
        slot = rem(y - target + 4, NY) - 1
        return rcopy(b_send.at[h], b_recv.at[h % 2, slot], b_ss.at[h], b_rs.at[h % 2, slot],
                     dev(x, (1 - c, h // 2), z, c))

    def fa_copy(h, k):
        return rcopy(fa_send.at[h, k], fa.at[y * 4 + zh], fa_ss.at[h, k], fa_rs.at[y * 4 + zh],
                     dev(x, (c, h // 2), zl + 2 * k, h % 2))

    def fa_self(h, k):
        return (y == c * 2 + h // 2) & (c == h % 2) & (zh == k)

    def fb_copy(h, d):
        xo, zo = (1 - rest_b if d // 4 else rest_b), zh_on[d % 4]
        q = xo * 4 + zo
        return rcopy(fb_send.at[h % 2, q], fb.at[rest_b * 4 + zh], fb_ss.at[h % 2, q],
                     fb_rs.at[rest_b * 4 + zh],
                     dev(x_b if d // 4 else x, here, zl + 2 * zo, h % 2))

    def b_owner(h):
        return y == (1 - c) * 2 + h // 2

    def spread(h):
        a_copy(h).wait_recv()
        total = a_send[h, pl.ds(rest_a * 4, 4)].astype(F32) + a_recv[h].astype(F32)
        fa_send[h] = total.astype(BF16)
        for k in range(4):
            @pl.when(fa_self(h, k))
            def _(k=k):
                fa[y * 4 + zh] = fa_send[h, k]

            @pl.when(jnp.logical_not(fa_self(h, k)))
            def _(k=k):
                fa_copy(h, k).start()

        @pl.when(b_owner(h))
        def _():
            for slot in range(3):
                rcopy(b_send.at[h], b_recv.at[h % 2, slot], b_ss.at[h], b_rs.at[h % 2, slot],
                      dev(x, over, z, c)).wait_recv()
            t = b_send[h].astype(F32)
            for slot in range(3):
                t = t + b_recv[h % 2, slot].astype(F32)
            fb_send[h % 2] = t.astype(BF16)
            for d in (6, 5, 7, 4, 2, 1, 3):
                fb_copy(h, d).start()

            @pl.when(c != h % 2)
            def _():
                fb_copy(h, 0).start()

            @pl.when(c == h % 2)
            def _():
                fb[rest_b * 4 + zh] = fb_send[h % 2, rest_b * 4 + zh]

    def finish():
        own_a = yh == c
        for s in range(16):
            @pl.when(jnp.logical_not(own_a & (y * 4 + zh == s)))
            def _(s=s):
                rcopy(fb_send.at[0, 0], fa.at[s], fb_ss.at[0, 0], fa_rs.at[s], sibling).wait_recv()
        for s in range(8):
            @pl.when(own_a | (rest_b * 4 + zh != s))
            def _(s=s):
                rcopy(fb_send.at[0, 0], fb.at[s], fb_ss.at[0, 0], fb_rs.at[s], sibling).wait_recv()
        ta = fa[0].astype(F32)
        for s in range(1, 16):
            ta = ta + fa[s].astype(F32)
        tb = fb[0].astype(F32)
        for s in range(1, 8):
            tb = tb + fb[s].astype(F32)
        ta = ta * (1.0 / 64.0)
        tb = tb * (1.0 / 64.0)
        w_ref[0] = jnp.where(yh == 0, ta, tb)
        w_ref[1] = jnp.where(yh == 0, tb, ta)

    attention(1)
    for t in range(2):
        x_copy(t, 0).wait()
        start(x_forward(t, 0))
    attention(2)
    attention(0)
    finalize(1)
    attention(3)
    finalize(2)
    finalize(0)
    for m in (2, 1, 3):
        for t in range(2):
            x_copy(t, m).wait_recv()
            start(x_forward(t, m))
    finalize(3)
    for m in range(4):
        for t in range(2):
            x_forward(t, m).wait_recv()
    pl.semaphore_wait(met, 5)
    for n, h in enumerate(ORDER):
        gathered(h)
        product(h)
        if n > 1:
            spread(ORDER[n - 2])
    spread(0)
    spread(3)
    for cp in sends:
        cp.wait_send()
    for h in range(KVH):
        for delta in (1, 2):
            @pl.when(sq + delta < 4)
            def _(h=h, delta=delta):
                kv_copy(h, delta).wait_send()

            @pl.when(sq >= delta)
            def _(h=h, delta=delta):
                part_copy(h, delta).wait_send()

        @pl.when(jnp.logical_not(b_owner(h)))
        def _(h=h):
            b_copy(h).wait_send()

        for k in range(4):
            @pl.when(jnp.logical_not(fa_self(h, k)))
            def _(h=h, k=k):
                fa_copy(h, k).wait_send()

        @pl.when(b_owner(h))
        def _(h=h):
            for d in range(1, 8):
                fb_copy(h, d).wait_send()

            @pl.when(c != h % 2)
            def _():
                fb_copy(h, 0).wait_send()
    finish()


def per_device(layer_input, query_states, key_states, value_states, output_grads, doc_lengths):
    hbm = pl.BlockSpec(memory_space=pltpu.HBM)
    vmem = pl.BlockSpec(memory_space=pltpu.VMEM)
    dma = pltpu.SemaphoreType.DMA
    dq, w = pl.pallas_call(
        kernel,
        out_shape=(
            jax.ShapeDtypeStruct((TOK, KVH * GROUP * HD), BF16),
            jax.ShapeDtypeStruct((2, ROWS, HD), F32),
        ),
        in_specs=[pl.BlockSpec(memory_space=pltpu.SMEM)] + [hbm] * 5,
        out_specs=(vmem, vmem),
        scratch_shapes=[
            pltpu.VMEM((TOK, D), BF16),
            pltpu.VMEM((TOK, KVH * GROUP * HD), BF16),
            pltpu.VMEM((TOK, KVH * GROUP * HD), BF16),
            pltpu.VMEM((KVH, 2, 3 * TOK, HD), BF16),
            pltpu.VMEM((TOK, 3 * TOK), F32),
            pltpu.VMEM((D, TOK), BF16),
            pltpu.VMEM((2, 8, 2, 4, ROWS, TOK), BF16),
            pltpu.VMEM((KVH, 2, HD, TOK), F32),
            pltpu.VMEM((KVH, 2, 2, HD, TOK), BF16),
            pltpu.VMEM((KVH, 2, 2, HD, TOK), BF16),
            pltpu.VMEM((KVH, 2, TOK, HD), BF16),
            pltpu.VMEM((2, KVH, 8 * TOK, HD), BF16),
            pltpu.VMEM((KVH, 8, ROWS, HD), BF16),
            pltpu.VMEM((KVH, 4, ROWS, HD), BF16),
            pltpu.VMEM((KVH, 8, ROWS, HD), BF16),
            pltpu.VMEM((2, 3, 8, ROWS, HD), BF16),
            pltpu.VMEM((KVH, 4, ROWS, HD), BF16),
            pltpu.VMEM((2, 8, ROWS, HD), BF16),
            pltpu.VMEM((16, ROWS, HD), BF16),
            pltpu.VMEM((8, ROWS, HD), BF16),
            dma((11,)),
            dma((KVH, 2)), dma((KVH, 2)),
            dma((2, 3)), dma((2, 3)), dma((2,)),
            dma((2, 4)), dma((2, 4)),
            dma((KVH, 2)), dma((KVH, 2)),
            dma((KVH, 2, 2, 4)), dma((KVH, 2, 4, 2)),
            dma((KVH,)), dma((KVH,)),
            dma((KVH,)), dma((2, 3)),
            dma((KVH, 4)), dma((16,)),
            dma((2, 8)), dma((8,)),
            pltpu.SemaphoreType.REGULAR,
        ],
        compiler_params=pltpu.CompilerParams(
            collective_id=0, has_side_effects=True, vmem_limit_bytes=40 * 1024 * 1024,
        ),
        cost_estimate=pl.CostEstimate(
            flops=2_600_000_000, bytes_accessed=4_000_000, transcendentals=1_000_000),
    )(pltpu.with_memory_space_constraint(doc_lengths, pltpu.HBM), *[pltpu.with_memory_space_constraint(a[0], pltpu.HBM) for a in (
        layer_input, query_states, key_states, value_states, output_grads)])
    return dq[None], w[0], w[1]


def solution(mesh):
    return jax.shard_map(
        per_device,
        mesh=mesh,
        in_specs=(
            P("dp", "seq", None),
            P("dp", "seq", None),
            P("dp", "seq", None),
            P("dp", "seq", None),
            P("dp", "seq", None),
            P("dp", None),
        ),
        out_specs=(P("dp", "seq", None), P("dp", "seq"), P("dp", "seq")),
        check_vma=False,
    )
```

```python
import jax
import jax.numpy as jnp
from jax import lax
from jax.experimental import pallas as pl
from jax.experimental.pallas import tpu as pltpu
from jax.sharding import PartitionSpec as P

HD = 128
KVH = 4
GROUP = 5
TOK = 128
D = 5120
XW = D // 4
NX, NY, NZ = 4, 4, 8
ORDER = (1, 2, 0, 3)
ROWS = 80
LOG2E = 1.4426950408889634
SCALE = HD ** (-0.5)
MESH = pl.DeviceIdType.MESH
F32 = jnp.float32
BF16 = jnp.bfloat16


def kernel(
    doc_ref, x_hbm, q_hbm, k_hbm, v_hbm, do_hbm,
    dq_ref, w_ref,
    xin, qin, doin, kv, bias, xt_send, xt_all,
    part_own, part_send, part_recv, kvout, kv_all, a_send, a_recv, b_send, b_recv,
    fa_send, fb_send, fa, fb,
    ld_sem, kv_ss, kv_rs, x_ss, x_rs, xl_sem, xf_ss, xf_rs, p_ss, p_rs,
    ag_ss, ag_rs, a_ss, a_rs, b_ss, b_rs, fa_ss, fa_rs, fb_ss, fb_rs, met,
):
    dp = lax.axis_index("dp")
    sq = lax.axis_index("seq")
    div, rem = lax.div, lax.rem
    x, z, yh = div(dp, 16), rem(div(dp, 2), 8), rem(dp, 2)
    yl, c = div(sq, 2), rem(sq, 2)
    y = yh * 2 + yl
    xl, v, zl, zh = rem(x, 2), div(x, 2), rem(z, 2), div(z, 2)
    u = xl + v - 2 * xl * v
    pair = (u, v)
    rest_a, rest_b = v + (u - v) * c, u + (v - u) * c
    x_next = (x + 1 - 2 * xl, rem(x + 3 + 2 * xl, NX))
    z_next = (z + 1 - 2 * zl, rem(z + 7 + 2 * zl, NZ))
    x_a = x_next[1] + (x_next[0] - x_next[1]) * c
    x_b = x_next[0] + (x_next[1] - x_next[0]) * c
    zh_on = [zh] + [rem(zh + k, 4) for k in (1, 2, 3)]
    z_on = [zl + 2 * k for k in zh_on]
    ranks = [sq] + [rem(sq + k, 4) for k in (1, 2, 3)]
    here, over, across, beyond = (yh, yl), (1 - yh, yl), (yh, 1 - yl), (1 - yh, 1 - yl)

    def member(t, m):
        return (x_next[t] if m // 2 else x), (z_next[t] if m % 2 else z)

    def dev(xx, yy, zz, cc):
        return (xx * 16 + zz * 2 + yy[0], yy[1] * 2 + cc)

    def seq_dev(delta):
        return (dp, ranks[delta])

    sibling = dev(x, here, z, 1 - c)

    def rcopy(src, dst, ss, rs, device):
        return pltpu.make_async_remote_copy(
            src_ref=src, dst_ref=dst, send_sem=ss, recv_sem=rs,
            device_id=device, device_id_type=MESH,
        )

    load_x = pltpu.make_async_copy(x_hbm, xin, ld_sem.at[8])
    load_q = pltpu.make_async_copy(q_hbm, qin, ld_sem.at[9])
    load_do = pltpu.make_async_copy(do_hbm, doin, ld_sem.at[10])
    loads = []
    for h in range(KVH):
        for i, ref in enumerate((k_hbm, v_hbm)):
            loads.append(pltpu.make_async_copy(
                ref.at[:, h * HD:(h + 1) * HD], kv.at[h, i, 256:384], ld_sem.at[h * 2 + i]))
    load_x.start()
    for cp in loads:
        cp.start()
    load_q.start()
    load_do.start()

    barrier = pltpu.get_barrier_semaphore()
    peers = [seq_dev(1), seq_dev(2), seq_dev(3)]
    for t in range(2):
        for m in (3, 2, 1):
            xx, zz = member(t, m)
            peers += [dev(xx, here, zz, c), dev(xx, here, zz, 1 - c)]
    for k in (1, 3, 0):
        zz = z_on[k]
        places = [(x, over), (x, beyond)]
        if k > 0:
            places = [(x, here)]
        for xx, yy in places:
            peers += [dev(xx, yy, zz, c), dev(xx, yy, zz, 1 - c)]
    for peer in peers:
        pl.semaphore_signal(barrier, inc=1, device_id=peer, device_id_type=MESH)

    def turn_block(ud, vd):
        def turn(i, _):
            to = pl.multiple_of((2 * ud + vd) * XW + i * 128, 128)
            at = pl.multiple_of((2 * vd + ud + vd - 2 * ud * vd) * XW + i * 128, 128)
            xt_send[pl.ds(to, 128), :] = xin[:, pl.ds(at, 128)].T
            return 0

        lax.fori_loop(0, XW // 128, turn, 0)

    def x_copy(t, m):
        xx, zz = member(t, m)
        xo, zo = (1 - pair[t] if m // 2 else pair[t]), (1 - zl if m % 2 else zl)
        view = xt_send.reshape(2, 2, 4, 2, 2, ROWS, TOK)
        src = view.at[:, xo, :, zo, t] if t else view.at[xo, :, :, zo, t]
        if m == 0:
            return pltpu.make_async_copy(src, xt_all.at[t, 0], xl_sem.at[t])
        return rcopy(src, xt_all.at[t, m * 2], x_ss.at[t, m - 1], x_rs.at[t, m - 1],
                     dev(xx, here, zz, c))

    def x_forward(t, m):
        return rcopy(xt_all.at[t, m * 2], xt_all.at[t, m * 2 + 1], xf_ss.at[t, m], xf_rs.at[t, m],
                     sibling)

    sends = []

    def start(cp):
        cp.start()
        sends.append(cp)

    for cp in loads:
        cp.wait()
    pl.semaphore_wait(barrier, len(peers))

    def kv_copy(h, delta):
        return rcopy(kv.at[h, :, 256:384], kv.at[h, :, (2 - delta) * TOK:(3 - delta) * TOK],
                     kv_ss.at[h, delta - 1], kv_rs.at[h, delta - 1], seq_dev(delta))

    for h in ORDER:
        for delta in (2, 1):
            @pl.when(sq + delta < 4)
            def _(h=h, delta=delta):
                kv_copy(h, delta).start()
    ahead, behind = dev(x, here, z_on[1], c), dev(x, here, z_on[3], c)
    close = [dev(xx, yy, z, c) for xx, yy in
             ((x, over), (x, beyond), (x, across), (x_next[0], here), (x_next[1], here))]
    for device in close + [ahead, behind]:
        pl.semaphore_signal(met.at[0], inc=1, device_id=device, device_id_type=MESH)
    for delta in (1, 2):
        @pl.when(sq < delta)
        def _(delta=delta):
            kv[:, :, (2 - delta) * TOK:(3 - delta) * TOK] = jnp.zeros((KVH, 2, TOK, HD), BF16)

        @pl.when(sq + delta > 3)
        def _(delta=delta):
            part_recv[:, delta - 1] = jnp.zeros((KVH, 2, HD, TOK), BF16)
    load_x.wait()
    turn_block(1 - u, v)
    turn_block(1 - u, 1 - v)
    start(x_copy(0, 3))
    start(x_copy(0, 2))
    turn_block(u, 1 - v)
    start(x_copy(1, 3))
    start(x_copy(1, 2))
    turn_block(u, v)
    for t in range(2):
        start(x_copy(t, 1))
        x_copy(t, 0).start()

    rows = lax.broadcasted_iota(jnp.int32, (TOK, 1), 0) + sq * TOK
    first = jnp.zeros((TOK, 1), jnp.int32)
    end = jnp.int32(0)
    for n in range(6):
        end = end + doc_ref[0, n]
        first = jnp.where(rows >= end, end, first)
    cols = lax.broadcasted_iota(jnp.int32, (TOK, 384), 1) + (sq - 2) * TOK
    bias[...] = jnp.where((cols >= first) & (cols <= rows), 0.0, -1e30).astype(F32)

    load_q.wait()
    load_do.wait()

    def part_copy(h, delta):
        return rcopy(part_send.at[h, delta - 1], part_recv.at[h, delta - 1],
                     p_ss.at[h, delta - 1], p_rs.at[h, delta - 1], seq_dev(4 - delta))

    def attention(h):
        for delta in (1, 2):
            @pl.when(sq >= delta)
            def _(delta=delta):
                kv_copy(h, delta).wait_recv()
        def stack(ref):
            return jnp.concatenate(
                [ref[:, (h * GROUP + g) * HD:(h * GROUP + g + 1) * HD] for g in range(GROUP)],
                axis=0)

        qs, dos = stack(qin), stack(doin)
        kk = kv[h, 0]
        nt = (((1,), (1,)), ((), ()))
        s = lax.dot_general(qs, kk, nt, preferred_element_type=F32).reshape(GROUP, TOK, 3 * TOK)
        dpr = lax.dot_general(dos, kv[h, 1], nt, preferred_element_type=F32)
        dpr = dpr.reshape(GROUP, TOK, 3 * TOK)
        s = s * (SCALE * LOG2E) + bias[...][None]
        m = jnp.max(s, axis=2, keepdims=True)
        e = jnp.exp2(s - m)
        p = e * (1.0 / jnp.sum(e, axis=2, keepdims=True))
        delta_r = jnp.sum(p * dpr, axis=2, keepdims=True)
        ds = (p * (dpr - delta_r) * SCALE).astype(BF16).reshape(GROUP * TOK, 3 * TOK)
        pb = p.astype(BF16).reshape(GROUP * TOK, 3 * TOK)
        tn = (((0,), (0,)), ((), ()))
        for i, (rows_in, grads) in enumerate(((qs, ds), (dos, pb))):
            t = lax.dot_general(rows_in, grads, tn, preferred_element_type=F32)
            part_own[h, i] = t[:, 256:384]
            part_send[h, 0, i] = t[:, 128:256].astype(BF16)
            part_send[h, 1, i] = t[:, 0:128].astype(BF16)
        for delta in (2, 1):
            @pl.when(sq >= delta)
            def _(delta=delta):
                part_copy(h, delta).start()
        dq = jnp.dot(ds, kk, preferred_element_type=F32).astype(BF16)
        for g in range(GROUP):
            dq_ref[:, (h * GROUP + g) * HD:(h * GROUP + g + 1) * HD] = dq[g * TOK:(g + 1) * TOK]

    def ag_copy(h, i, t, m):
        rel = 1 - c if i else c
        rows_ = pl.ds(pl.multiple_of((m * 2 + rel) * TOK, TOK), TOK)
        xx, zz = member(t, m)
        return rcopy(kvout.at[h, i], kv_all.at[t, h, rows_], ag_ss.at[h, i, t, m],
                     ag_rs.at[h, t, m, rel], dev(xx, here, zz, i))

    def ag_sibling(h, t):
        return rcopy(kvout.at[h, 1 - c], kv_all.at[t, h, TOK:2 * TOK],
                     ag_ss.at[h, 0, t, 0], ag_rs.at[h, t, 0, 1], sibling)

    def finalize(h):
        for delta in (1, 2):
            @pl.when(sq + delta < 4)
            def _(delta=delta):
                part_copy(h, delta).wait_recv()
        for i in range(2):
            total = (part_own[h, i] + part_recv[h, 0, i].astype(F32)
                     + part_recv[h, 1, i].astype(F32))
            kvout[h, i] = total.T.astype(BF16)
        for m in (3, 2, 1):
            for t in range(2):
                for i in range(2):
                    start(ag_copy(h, i, t, m))
        for t in range(2):
            start(ag_sibling(h, t))
            kv_all[t, h, 0:TOK] = kvout[h, c]

    def gathered(h):
        for t in range(2):
            ag_sibling(h, t).wait_recv()
            for m in (1, 2, 3):
                for rel in range(2):
                    rcopy(kvout.at[h, 0], kv_all.at[t, h, 0:TOK], ag_ss.at[h, 0, 0, 0],
                          ag_rs.at[h, t, m, rel], sibling).wait_recv()

    HALF = 8 * ROWS

    def product(h):
        for part in range(2):
            t = c if part == 0 else 1 - c
            send = a_send if part == 0 else b_send
            for n in range(2):
                w = jnp.concatenate(
                    [xt_all[t, s, n].reshape(4 * ROWS, TOK) for s in range(8)],
                    axis=1)
                out = jnp.dot(w, kv_all[t, h], preferred_element_type=F32)
                send[h, n * 4:(n + 1) * 4] = out.reshape(4, ROWS, HD).astype(BF16)
            if part == 0:
                start(a_copy(h))
            else:
                @pl.when(y != (1 - c) * 2 + h // 2)
                def _():
                    b_copy(h).start()

    def a_copy(h):
        src = a_send.reshape(KVH, 2, 4, ROWS, HD).at[h, 1 - rest_a]
        return rcopy(src, a_recv.at[h], a_ss.at[h], a_rs.at[h], dev(x_a, here, z, c))

    def b_copy(h):
        target = (1 - c) * 2 + h // 2
        slot = rem(y - target + 4, NY) - 1
        return rcopy(b_send.at[h], b_recv.at[h % 2, slot], b_ss.at[h], b_rs.at[h % 2, slot],
                     dev(x, (1 - c, h // 2), z, c))

    def fa_copy(h, k):
        return rcopy(fa_send.at[h, k], fa.at[y * 4 + zh], fa_ss.at[h, k], fa_rs.at[y * 4 + zh],
                     dev(x, (c, h // 2), zl + 2 * k, h % 2))

    def fa_self(h, k):
        return (y == c * 2 + h // 2) & (c == h % 2) & (zh == k)

    def fb_copy(h, d):
        xo, zo = (1 - rest_b if d // 4 else rest_b), zh_on[d % 4]
        q = xo * 4 + zo
        return rcopy(fb_send.at[h % 2, q], fb.at[rest_b * 4 + zh], fb_ss.at[h % 2, q],
                     fb_rs.at[rest_b * 4 + zh],
                     dev(x_b if d // 4 else x, here, zl + 2 * zo, h % 2))

    def b_owner(h):
        return y == (1 - c) * 2 + h // 2

    def spread(h):
        a_copy(h).wait_recv()
        total = a_send[h, pl.ds(rest_a * 4, 4)].astype(F32) + a_recv[h].astype(F32)
        fa_send[h] = total.astype(BF16)
        for k in range(4):
            @pl.when(fa_self(h, k))
            def _(k=k):
                fa[y * 4 + zh] = fa_send[h, k]

            @pl.when(jnp.logical_not(fa_self(h, k)))
            def _(k=k):
                fa_copy(h, k).start()

        @pl.when(b_owner(h))
        def _():
            for slot in range(3):
                rcopy(b_send.at[h], b_recv.at[h % 2, slot], b_ss.at[h], b_rs.at[h % 2, slot],
                      dev(x, over, z, c)).wait_recv()
            t = b_send[h].astype(F32)
            for slot in range(3):
                t = t + b_recv[h % 2, slot].astype(F32)
            fb_send[h % 2] = t.astype(BF16)
            for d in (6, 5, 7, 4, 2, 1, 3):
                fb_copy(h, d).start()

            @pl.when(c != h % 2)
            def _():
                fb_copy(h, 0).start()

            @pl.when(c == h % 2)
            def _():
                fb[rest_b * 4 + zh] = fb_send[h % 2, rest_b * 4 + zh]

    def finish():
        own_a = yh == c
        for s in range(16):
            @pl.when(jnp.logical_not(own_a & (y * 4 + zh == s)))
            def _(s=s):
                rcopy(fb_send.at[0, 0], fa.at[s], fb_ss.at[0, 0], fa_rs.at[s], sibling).wait_recv()
        for s in range(8):
            @pl.when(own_a | (rest_b * 4 + zh != s))
            def _(s=s):
                rcopy(fb_send.at[0, 0], fb.at[s], fb_ss.at[0, 0], fb_rs.at[s], sibling).wait_recv()
        ta = fa[0].astype(F32)
        for s in range(1, 16):
            ta = ta + fa[s].astype(F32)
        tb = fb[0].astype(F32)
        for s in range(1, 8):
            tb = tb + fb[s].astype(F32)
        ta = ta * (1.0 / 64.0)
        tb = tb * (1.0 / 64.0)
        w_ref[0] = jnp.where(yh == 0, ta, tb)
        w_ref[1] = jnp.where(yh == 0, tb, ta)

    attention(1)
    for t in range(2):
        x_copy(t, 0).wait()
        start(x_forward(t, 0))
    attention(2)
    attention(0)
    pl.semaphore_wait(met.at[0], 7)
    for device in (ahead, behind):
        pl.semaphore_signal(met.at[1], inc=1, device_id=device, device_id_type=MESH)
    finalize(1)
    attention(3)
    finalize(2)
    finalize(0)
    finalize(3)
    for m in (2, 1, 3):
        for t in range(2):
            x_copy(t, m).wait_recv()
            start(x_forward(t, m))
    for m in range(4):
        for t in range(2):
            x_forward(t, m).wait_recv()
    pl.semaphore_wait(met.at[1], 2)
    for n, h in enumerate(ORDER):
        gathered(h)
        product(h)
        if n > 1:
            spread(ORDER[n - 2])
    spread(0)
    spread(3)
    for cp in sends:
        cp.wait_send()
    for h in range(KVH):
        for delta in (1, 2):
            @pl.when(sq + delta < 4)
            def _(h=h, delta=delta):
                kv_copy(h, delta).wait_send()

            @pl.when(sq >= delta)
            def _(h=h, delta=delta):
                part_copy(h, delta).wait_send()

        @pl.when(jnp.logical_not(b_owner(h)))
        def _(h=h):
            b_copy(h).wait_send()

        for k in range(4):
            @pl.when(jnp.logical_not(fa_self(h, k)))
            def _(h=h, k=k):
                fa_copy(h, k).wait_send()

        @pl.when(b_owner(h))
        def _(h=h):
            for d in range(1, 8):
                fb_copy(h, d).wait_send()

            @pl.when(c != h % 2)
            def _():
                fb_copy(h, 0).wait_send()
    finish()


def per_device(layer_input, query_states, key_states, value_states, output_grads, doc_lengths):
    hbm = pl.BlockSpec(memory_space=pltpu.HBM)
    vmem = pl.BlockSpec(memory_space=pltpu.VMEM)
    dma = pltpu.SemaphoreType.DMA
    dq, w = pl.pallas_call(
        kernel,
        out_shape=(
            jax.ShapeDtypeStruct((TOK, KVH * GROUP * HD), BF16),
            jax.ShapeDtypeStruct((2, ROWS, HD), F32),
        ),
        in_specs=[pl.BlockSpec(memory_space=pltpu.SMEM)] + [hbm] * 5,
        out_specs=(vmem, vmem),
        scratch_shapes=[
            pltpu.VMEM((TOK, D), BF16),
            pltpu.VMEM((TOK, KVH * GROUP * HD), BF16),
            pltpu.VMEM((TOK, KVH * GROUP * HD), BF16),
            pltpu.VMEM((KVH, 2, 3 * TOK, HD), BF16),
            pltpu.VMEM((TOK, 3 * TOK), F32),
            pltpu.VMEM((D, TOK), BF16),
            pltpu.VMEM((2, 8, 2, 4, ROWS, TOK), BF16),
            pltpu.VMEM((KVH, 2, HD, TOK), F32),
            pltpu.VMEM((KVH, 2, 2, HD, TOK), BF16),
            pltpu.VMEM((KVH, 2, 2, HD, TOK), BF16),
            pltpu.VMEM((KVH, 2, TOK, HD), BF16),
            pltpu.VMEM((2, KVH, 8 * TOK, HD), BF16),
            pltpu.VMEM((KVH, 8, ROWS, HD), BF16),
            pltpu.VMEM((KVH, 4, ROWS, HD), BF16),
            pltpu.VMEM((KVH, 8, ROWS, HD), BF16),
            pltpu.VMEM((2, 3, 8, ROWS, HD), BF16),
            pltpu.VMEM((KVH, 4, ROWS, HD), BF16),
            pltpu.VMEM((2, 8, ROWS, HD), BF16),
            pltpu.VMEM((16, ROWS, HD), BF16),
            pltpu.VMEM((8, ROWS, HD), BF16),
            dma((11,)),
            dma((KVH, 2)), dma((KVH, 2)),
            dma((2, 3)), dma((2, 3)), dma((2,)),
            dma((2, 4)), dma((2, 4)),
            dma((KVH, 2)), dma((KVH, 2)),
            dma((KVH, 2, 2, 4)), dma((KVH, 2, 4, 2)),
            dma((KVH,)), dma((KVH,)),
            dma((KVH,)), dma((2, 3)),
            dma((KVH, 4)), dma((16,)),
            dma((2, 8)), dma((8,)),
            pltpu.SemaphoreType.REGULAR((2,)),
        ],
        compiler_params=pltpu.CompilerParams(
            collective_id=0, has_side_effects=True, vmem_limit_bytes=40 * 1024 * 1024,
        ),
        cost_estimate=pl.CostEstimate(
            flops=2_600_000_000, bytes_accessed=4_000_000, transcendentals=1_000_000),
    )(pltpu.with_memory_space_constraint(doc_lengths, pltpu.HBM), *[pltpu.with_memory_space_constraint(a[0], pltpu.HBM) for a in (
        layer_input, query_states, key_states, value_states, output_grads)])
    return dq[None], w[0], w[1]


def solution(mesh):
    return jax.shard_map(
        per_device,
        mesh=mesh,
        in_specs=(
            P("dp", "seq", None),
            P("dp", "seq", None),
            P("dp", "seq", None),
            P("dp", "seq", None),
            P("dp", "seq", None),
            P("dp", None),
        ),
        out_specs=(P("dp", "seq", None), P("dp", "seq"), P("dp", "seq")),
        check_vma=False,
    )
```
